256 devices in a mesh: row: 16 (over y, z_lo), col: 8 (over x, z_hi), depth: 2 (over core).
Axes of the slice: x: 4, y: 4, z: 8 (z_hi: 2, z_lo: 4; z = z_hi * 4 + z_lo), core: 2. Of those that a mesh axis runs over, the one named last changes fastest.
Arguments:
- pair: bfloat16 [512, 512, 128], P('row', ('col', 'depth')), may hold values from -6 to 6
- grad_out: bfloat16 [512, 512, 128], P('row', ('col', 'depth')), may hold values from -6 to 6
- pair_mask: int32 [512, 512], P('row', ('col', 'depth')), may hold values 0 or 1
- ln_in_gain: float32 [128], replicated, may hold values from 0.5 to 1.5
- ln_in_bias: float32 [128], replicated, may hold values from -3 to 3
- in_proj: bfloat16 [128, 512], replicated, may hold values from -0.5 to 0.5
- w_gate: bfloat16 [128, 128], replicated, may hold values from -0.5 to 0.5
- inner_norm_gain: float32 [128], replicated, may hold values from 0.5 to 1.5
- inner_norm_bias: float32 [128], replicated, may hold values from -3 to 3
- w_out: bfloat16 [128, 128], replicated, may hold values from -0.5 to 0.5
Outputs:
- grad_pair: bfloat16 [512, 512, 128], P('row', ('col', 'depth'))
- grad_in_proj: float32 [128, 512], replicated
- grad_w_gate: float32 [128, 128], replicated
- grad_w_out: float32 [128, 128], replicated
- grad_ln_in: float32 [2, 128], replicated
- inner_norm_gradients: float32 [2, 128], replicated
The draws below stay inside these ranges and needn't reach their ends.
All inputs are finite; a program needn't handle non-finite values. No bound on the sum of `pair_mask` on one device may be relied on, other than what follows from the above.
Results may differ from the reference program's by a relative error of at most 0.02.
Values may be sent and summed in bfloat16 or wider, within the bound.
No kernel may reach another device: no remote copies, remote signals or barrier semaphores. Data moves between devices by JAX's collectives and lax.ppermute only.
A program may use at most 64 MiB of HBM per device.

```python
import jax
import jax.numpy as jnp
from jax import lax

C = 128
H = 128
TILE = 32
TOKENS = 512
N_ROW = 16


def with_ends(entries, key, least, largest):
    longest = entries.shape.index(max(entries.shape))
    spots = []
    for shift in (0, 1):
        where = [jax.random.randint(jax.random.fold_in(key, axis), (), 0, length) for axis, length in enumerate(entries.shape)]
        where[longest] = (where[longest] + shift) % entries.shape[longest]
        spots.append(tuple(where))
    return entries.at[spots[0]].set(least).at[spots[1]].set(largest)


def steps_of(own_key, dims, shards, low, high):
    level = 1.0
    for dim, blocks in shards:
        steps = jax.random.uniform(jax.random.fold_in(jax.random.fold_in(own_key, 6), dim), (blocks,), jnp.float32, low / len(shards), high / len(shards))
        level = level * jnp.repeat(jnp.exp(steps), dims[dim] // blocks).reshape((-1,) + (1,) * (len(dims) - 1 - dim))
    return level


def noise(own_key, shape, width, limit, split=(), held_as=jnp.bfloat16):
    factor_of = steps_of(own_key, shape, split, -0.22, 0.18) if split else 1.0
    drawn = jax.random.normal(own_key, shape, jnp.float32) * width * factor_of
    return jnp.minimum(jnp.maximum(drawn, -limit), limit).astype(held_as)


def setup_inputs(seed: int = 0) -> dict:
    key_list = jax.random.split(jax.random.key(seed), 11)
    return {
        "pair": noise(key_list[0], (TOKENS, TOKENS, C), 1.0, 6.0, ((0, 16), (1, 16))),
        "grad_out": noise(key_list[1], (TOKENS, TOKENS, C), 1.0, 6.0, ((0, 16), (1, 16))),
        "pair_mask": with_ends((jax.random.randint(key_list[2], (TOKENS, TOKENS), 0, 8) < 7).astype(jnp.int32), jax.random.fold_in(key_list[2], 1), 0, 1),
        "ln_in_gain": jnp.clip(1.0 + 0.1 * jax.random.normal(key_list[3], (C,), jnp.float32), 0.5, 1.5),
        "ln_in_bias": noise(key_list[4], (C,), 0.5, 3.0, (), jnp.float32),
        "in_proj": noise(key_list[5], (C, 4 * H), C ** -0.5, 0.5),
        "w_gate": noise(key_list[6], (C, C), C ** -0.5, 0.5),
        "inner_norm_gain": jnp.clip(1.0 + 0.1 * jax.random.normal(key_list[7], (H,), jnp.float32), 0.5, 1.5),
        "inner_norm_bias": noise(key_list[8], (H,), 0.5, 3.0, (), jnp.float32),
        "w_out": noise(key_list[9], (H, C), H ** -0.5, 0.5),
    }


def layer_norm_forward(value, gain, bias):
    centre = value - lax.optimization_barrier(jnp.mean(value, axis=-1, keepdims=True))
    inverse = lax.rsqrt(lax.optimization_barrier(jnp.mean(centre * centre, axis=-1, keepdims=True)) + 1e-05)
    scaled = centre * inverse
    return (scaled * gain + bias, scaled, inverse)

def layer_norm_backward(grad, scaled, inverse, gain):
    tangent = grad * gain
    first = lax.optimization_barrier(jnp.mean(tangent, axis=-1, keepdims=True))
    second = lax.optimization_barrier(jnp.mean(tangent * scaled, axis=-1, keepdims=True))
    return inverse * (tangent - first - scaled * second)

def reference(pair, grad_out, pair_mask, ln_in_gain, ln_in_bias, in_proj, w_gate, inner_norm_gain, inner_norm_bias, w_out):
    token_count = pair.shape[0]
    chans = pair.shape[2]
    hidden_width = w_out.shape[0]
    cells = token_count * token_count
    zf = pair.astype(jnp.float32).reshape(cells, chans)
    zn, zhat, zinv = layer_norm_forward(zf, ln_in_gain, ln_in_bias)
    normed = zn.astype(jnp.bfloat16)
    proj = jnp.dot(normed, in_proj, preferred_element_type=jnp.float32)
    maskf = pair_mask.astype(jnp.float32).reshape(cells, 1)
    a_val = proj[:, :hidden_width]
    sig_a = jax.nn.sigmoid(proj[:, hidden_width:2 * hidden_width])
    b_val = proj[:, 2 * hidden_width:3 * hidden_width]
    sig_b = jax.nn.sigmoid(proj[:, 3 * hidden_width:])
    left = (sig_a * a_val * maskf).astype(jnp.bfloat16).reshape(token_count, token_count, hidden_width)
    right = (sig_b * b_val * maskf).astype(jnp.bfloat16).reshape(token_count, token_count, hidden_width)
    left_f = left.astype(jnp.float32)
    right_f = right.astype(jnp.float32)
    inner_product = jnp.einsum('ikh,jkh->ijh', left_f, right_f, precision=lax.Precision.HIGHEST).reshape(cells, hidden_width)
    normalised_input, centred_scaled_input, inverse_deviation = layer_norm_forward(inner_product, inner_norm_gain, inner_norm_bias)
    xnorm = normalised_input.astype(jnp.bfloat16)
    outp = jnp.dot(xnorm, w_out, preferred_element_type=jnp.float32)
    gate = jax.nn.sigmoid(jnp.dot(normed, w_gate, preferred_element_type=jnp.float32))
    upstream = grad_out.astype(jnp.float32).reshape(cells, chans)
    d_out_proj = (upstream * gate).astype(jnp.bfloat16)
    d_gate_pre = (upstream * outp * gate * (1.0 - gate)).astype(jnp.bfloat16)
    normed_input_grad = jnp.dot(d_out_proj, w_out.T, preferred_element_type=jnp.float32)
    grad_w_out = jnp.dot(xnorm.T, d_out_proj, preferred_element_type=jnp.float32)
    inner_norm_gradients = jnp.stack([lax.optimization_barrier(jnp.sum(normed_input_grad * centred_scaled_input, axis=0)), lax.optimization_barrier(jnp.sum(normed_input_grad, axis=0))])
    input_gradient = layer_norm_backward(normed_input_grad, centred_scaled_input, inverse_deviation, inner_norm_gain).astype(jnp.bfloat16).reshape(token_count, token_count, hidden_width)
    grad_xf = input_gradient.astype(jnp.float32)
    grad_a = jnp.einsum('ijh,jkh->ikh', grad_xf, right_f, precision=lax.Precision.HIGHEST).reshape(cells, hidden_width)
    total = jnp.zeros((token_count, token_count, hidden_width), jnp.float32)
    for tile_index in range(N_ROW):
        lower = tile_index * TILE
        term = jnp.einsum('ijh,ikh->jkh', grad_xf[lower:lower + TILE], left_f[lower:lower + TILE], precision=lax.Precision.HIGHEST)
        rounded = lax.optimization_barrier(term.astype(jnp.bfloat16))
        total = total + rounded.astype(jnp.float32)
    grad_b = total.astype(jnp.bfloat16).astype(jnp.float32).reshape(cells, hidden_width)
    d_proj = jnp.concatenate([grad_a * sig_a * maskf, grad_a * a_val * maskf * sig_a * (1.0 - sig_a), grad_b * sig_b * maskf, grad_b * b_val * maskf * sig_b * (1.0 - sig_b)], axis=1).astype(jnp.bfloat16)
    grad_in_proj = jnp.dot(normed.T, d_proj, preferred_element_type=jnp.float32)
    grad_w_gate = jnp.dot(normed.T, d_gate_pre, preferred_element_type=jnp.float32)
    d_normed = jnp.dot(d_proj, in_proj.T, preferred_element_type=jnp.float32) + jnp.dot(d_gate_pre, w_gate.T, preferred_element_type=jnp.float32)
    grad_ln_in = jnp.stack([lax.optimization_barrier(jnp.sum(d_normed * zhat, axis=0)), lax.optimization_barrier(jnp.sum(d_normed, axis=0))])
    grad_pair = layer_norm_backward(d_normed, zhat, zinv, ln_in_gain).astype(jnp.bfloat16).reshape(token_count, token_count, chans)
    return (grad_pair, grad_in_proj, grad_w_gate, grad_w_out, grad_ln_in, inner_norm_gradients)
```

```python
import jax
import jax.numpy as jnp
from jax import lax
from jax.experimental import pallas as pl
from jax.experimental.pallas import tpu as pltpu
from jax.sharding import PartitionSpec as P

F32 = jnp.float32
BF16 = jnp.bfloat16
PLANE = ("row", "col")
T = 32
CH = 128
CELLS = T * T
SUB = 8
GROUPS = T // SUB


def call(kernel, out_shapes, *args, scratch=(), flops=2_000_000, smem=()):
    specs = [
        pl.BlockSpec(memory_space=pltpu.SMEM) if i in smem else pl.BlockSpec(memory_space=pltpu.VMEM)
        for i in range(len(args))
    ]
    moved = sum(a.size * a.dtype.itemsize for a in args)
    moved += sum(o.size * o.dtype.itemsize for o in out_shapes)
    return pl.pallas_call(
        kernel,
        out_shape=out_shapes,
        in_specs=specs,
        out_specs=[pl.BlockSpec(memory_space=pltpu.VMEM) for _ in out_shapes],
        scratch_shapes=list(scratch),
        compiler_params=pltpu.CompilerParams(vmem_limit_bytes=40 * 1024 * 1024),
        cost_estimate=pl.CostEstimate(flops=flops, bytes_accessed=moved, transcendentals=0),
    )(*args)


def struct(shape, dtype):
    return jax.ShapeDtypeStruct(shape, dtype)


def column(row):
    return jnp.transpose(jnp.broadcast_to(row, (CH, CH)))[:, :1]


def dot(a, b, ca, cb):
    return lax.dot_general(a, b, (((ca,), (cb,)), ((), ())), preferred_element_type=F32)


def channel_major(ref):
    chunks = []
    for s in range(SUB):
        block = jnp.concatenate([ref[SUB * g + s] for g in range(GROUPS)], axis=0)
        chunks.append(jnp.transpose(block.astype(F32)))
    return jnp.concatenate(chunks, axis=1)


def to_tiles(value, scratch, first, stride):
    for s in range(SUB):
        scratch[pl.ds(first + s, CH, stride=stride), :] = value[:, s * CH : (s + 1) * CH]


def from_tiles(scratch, first, stride):
    return jnp.concatenate(
        [scratch[pl.ds(first + s, CH, stride=stride), :] for s in range(SUB)], axis=1
    )


def norm(value):
    centre = value - jnp.mean(value, axis=0, keepdims=True)
    inverse = lax.rsqrt(jnp.mean(centre * centre, axis=0, keepdims=True) + 1e-05)
    return centre * inverse, inverse


def norm_back(grad, scaled, inverse, gain):
    tangent = grad * gain
    first = jnp.mean(tangent, axis=0, keepdims=True)
    second = jnp.mean(tangent * scaled, axis=0, keepdims=True)
    return inverse * (tangent - first - scaled * second)


def swap_groups(parts):
    a, b, c, d = parts
    axis = a.ndim - 1
    lane = lax.broadcasted_iota(jnp.int32, a.shape, axis)
    low = lane < 64
    even = (lane & 32) == 0
    a, c = jnp.where(low, a, pltpu.roll(c, 64, axis)), jnp.where(low, pltpu.roll(a, 64, axis), c)
    b, d = jnp.where(low, b, pltpu.roll(d, 64, axis)), jnp.where(low, pltpu.roll(b, 64, axis), d)
    a, b = jnp.where(even, a, pltpu.roll(b, 32, axis)), jnp.where(even, pltpu.roll(a, 96, axis), b)
    c, d = jnp.where(even, c, pltpu.roll(d, 32, axis)), jnp.where(even, pltpu.roll(c, 96, axis), d)
    return a, b, c, d


def to_matrix(tiles):
    blocks = tiles.shape[0]
    halves = []
    for half in range(2):
        parts = [tiles[:, half * 4 + part].astype(F32) for part in range(4)]
        rows = jnp.stack(swap_groups(parts), axis=1)
        halves.append(rows.reshape(blocks * T, CH))
    return jnp.concatenate(halves, axis=1)


def from_matrix(matrix):
    blocks = matrix.shape[0] // T
    parts = []
    for half in range(2):
        rows = matrix[:, half * CH : (half + 1) * CH].reshape(blocks, GROUPS, SUB, CH)
        parts += list(swap_groups([rows[:, g] for g in range(GROUPS)]))
    return jnp.stack(parts, axis=1)


def factors_kernel(pair, mask, gain, bias, in_proj, send, normed, zhat, zinv, coef, scratch):
    scaled, inverse = norm(channel_major(pair))
    zhat[...] = scaled
    zinv[...] = inverse
    value = (scaled * column(gain[...]) + column(bias[...])).astype(BF16)
    normed[...] = value
    proj = dot(in_proj[...], value, 0, 0)
    flags = mask[...].astype(F32)
    tile = jnp.concatenate([flags[SUB * g : SUB * (g + 1)] for g in range(GROUPS)], axis=1)
    m = jnp.concatenate([tile[s : s + 1] for s in range(SUB)], axis=1)
    for side in range(2):
        val = proj[2 * side * CH : (2 * side + 1) * CH]
        sig = jax.nn.sigmoid(proj[(2 * side + 1) * CH : (2 * side + 2) * CH])
        gated = sig * m
        factor = gated * val
        to_tiles(factor, scratch, side * SUB, 2 * SUB)
        coef[2 * side * CH : (2 * side + 1) * CH] = gated
        coef[(2 * side + 1) * CH : (2 * side + 2) * CH] = factor * (1.0 - sig)
    send[...] = scratch[...].reshape(CH, 2 * SUB, CH).astype(BF16)


def gate_kernel(grad_out, normed, w_gate, w_out, d_out_proj, d_xnorm, slope):
    upstream = channel_major(grad_out)
    gate = jax.nn.sigmoid(dot(w_gate[...], normed[...], 0, 0))
    moved = upstream * gate
    slope[...] = moved * (1.0 - gate)
    rounded = moved.astype(BF16)
    d_out_proj[...] = rounded
    d_xnorm[...] = dot(w_out[...], rounded, 1, 0)


def product_kernel(parity, own, other, send, left_own, right_own):
    rows = lax.bitwise_and(parity[0], 1)
    left_a = to_matrix(own[:, :, :, :SUB].reshape(16, 8, SUB, CH)).astype(BF16)
    left_b = to_matrix(other[:, :, :, :SUB].reshape(16, 8, SUB, CH)).astype(BF16)
    right_a = to_matrix(own[:, :, :, SUB:].reshape(16, 8, SUB, CH)).astype(BF16)
    left_own[...] = left_a
    right_own[...] = right_a
    mine = to_matrix(own[:, pl.ds(rows, 1), :, SUB:].reshape(8, 8, SUB, CH)).astype(BF16)
    theirs = to_matrix(other[:, pl.ds(rows, 1), :, SUB:].reshape(8, 8, SUB, CH)).astype(BF16)
    x = dot(left_a, mine, 1, 1) + dot(left_b, theirs, 1, 1)
    send[...] = from_matrix(x).reshape(CH, SUB, CH).astype(BF16)


def inner_kernel(recv, d_xnorm, gain, send, xhat, scratch):
    scratch[...] = recv[...].astype(F32).reshape(CELLS, CH)
    scaled, inverse = norm(from_tiles(scratch, 0, SUB))
    xhat[...] = scaled
    to_tiles(norm_back(d_xnorm[...], scaled, inverse, column(gain[...])), scratch, 0, SUB)
    send[...] = scratch[...].reshape(CH, SUB, CH).astype(BF16)


def sums(first, second, place):
    lane = lax.broadcasted_iota(jnp.int32, (CH, CH), 1)
    a = jnp.sum(first, axis=1, keepdims=True)
    b = jnp.sum(second, axis=1, keepdims=True)
    return jnp.where(lane == place, a, jnp.where(lane == place + 1, b, 0.0))


def output_kernel(
    xhat, d_xnorm, slope, d_out_proj, normed, gain, bias, w_out, w_gate, g_gate, g_out, inner, partial
):
    scaled = xhat[...]
    xnorm = (scaled * column(gain[...]) + column(bias[...])).astype(BF16)
    outp = dot(w_out[...], xnorm, 0, 0)
    d_gate_pre = (slope[...] * outp).astype(BF16)
    g_out[...] = dot(xnorm, d_out_proj[...], 1, 1)
    g_gate[...] = dot(normed[...], d_gate_pre, 1, 1)
    partial[...] = dot(w_gate[...], d_gate_pre, 1, 0)
    grad = d_xnorm[...]
    inner[...] = sums(grad * scaled, grad, 2)


def back_kernel(parity, own, other, left, right, send):
    flip = lax.bitwise_and(parity[0], 1) == 1
    mine = to_matrix(own[...].reshape(16, 8, SUB, CH)).astype(BF16)
    theirs = to_matrix(other[...].reshape(16, 8, SUB, CH)).astype(BF16)
    even = jnp.where(flip, theirs, mine)
    odd = jnp.where(flip, mine, theirs)
    pairs = right[...].reshape(8, 2, T, 2 * CH)
    da = dot(even, pairs[:, 0].reshape(8 * T, 2 * CH), 1, 0)
    da += dot(odd, pairs[:, 1].reshape(8 * T, 2 * CH), 1, 0)
    db_even = dot(even, left[...], 0, 0).reshape(8, T, 2 * CH)
    db_odd = dot(odd, left[...], 0, 0).reshape(8, T, 2 * CH)
    db = jnp.stack([db_even, db_odd], axis=1).reshape(16 * T, 2 * CH)
    both = jnp.concatenate([from_matrix(da), from_matrix(db)], axis=2)
    send[...] = both.reshape(CH, 2 * SUB, CH).astype(BF16)


def project_kernel(
    recv, coef, normed, zhat, partial, in_proj, g_gate, g_out, inner, send, d_normed, scratch, packed
):
    scratch[...] = recv[...].astype(F32).reshape(2 * CELLS, CH)
    da = from_tiles(scratch, 0, 2 * SUB)
    db = from_tiles(scratch, SUB, 2 * SUB)
    d_proj = jnp.concatenate(
        [
            (da * coef[0:CH]).astype(BF16),
            (da * coef[CH : 2 * CH]).astype(BF16),
            (db * coef[2 * CH : 3 * CH]).astype(BF16),
            (db * coef[3 * CH :]).astype(BF16),
        ],
        axis=0,
    )
    g_in = dot(normed[...], d_proj, 1, 1)
    grad = dot(in_proj[...], d_proj, 1, 0) + partial[...]
    d_normed[...] = grad
    for part in range(4):
        packed[pl.ds(part, CH, stride=SUB), :] = g_in[:, part * CH : (part + 1) * CH]
    packed[pl.ds(4, CH, stride=SUB), :] = g_gate[...]
    packed[pl.ds(5, CH, stride=SUB), :] = g_out[...]
    packed[pl.ds(6, CH, stride=SUB), :] = inner[...] + sums(grad * zhat[...], grad, 0)
    packed[pl.ds(7, CH, stride=SUB), :] = jnp.zeros((CH, CH), F32)
    send[...] = packed[...].reshape(CH, SUB, CH)


def pair_kernel(d_normed, zhat, zinv, gain, out):
    grad = norm_back(d_normed[...], zhat[...], zinv[...], column(gain[...]))
    for s in range(SUB):
        block = jnp.transpose(grad[:, s * CH : (s + 1) * CH]).astype(BF16)
        for g in range(GROUPS):
            out[SUB * g + s] = block[g * T : (g + 1) * T]


def total_kernel(recv, send):
    total = jnp.sum(recv[...], axis=0, keepdims=True)
    send[...] = jnp.broadcast_to(total, (CH, SUB, CH))


def unpack_kernel(own, other, g_in, g_gate, g_out, ln_in, inner, scratch):
    scratch[...] = (own[...] + other[...]).reshape(CELLS, CH)
    for part in range(4):
        g_in[:, part * CH : (part + 1) * CH] = scratch[pl.ds(part, CH, stride=SUB), :]
    g_gate[...] = scratch[pl.ds(4, CH, stride=SUB), :]
    g_out[...] = scratch[pl.ds(5, CH, stride=SUB), :]
    norms = jnp.transpose(scratch[pl.ds(6, CH, stride=SUB), :])
    ln_in[...] = norms[0:2]
    inner[...] = norms[2:4]


def swap_cores(value):
    return lax.ppermute(value, "depth", [(0, 1), (1, 0)])


def exchange(value):
    return lax.all_to_all(value, PLANE, 0, 0, tiled=True)


def per_device(
    pair,
    grad_out,
    pair_mask,
    ln_in_gain,
    ln_in_bias,
    in_proj,
    w_gate,
    inner_norm_gain,
    inner_norm_bias,
    w_out,
):
    parity = lax.axis_index("depth").astype(jnp.int32).reshape(1)
    in_gain = ln_in_gain.reshape(1, CH)
    in_bias = ln_in_bias.reshape(1, CH)
    x_gain = inner_norm_gain.reshape(1, CH)
    x_bias = inner_norm_bias.reshape(1, CH)
    one = struct((CH, SUB, CH), BF16)
    two = struct((CH, 2 * SUB, CH), BF16)
    wide = struct((CH, CELLS), F32)
    square = struct((CH, CH), F32)

    factors, normed, zhat, zinv, coef = call(
        factors_kernel,
        [two, struct((CH, CELLS), BF16), wide, struct((1, CELLS), F32), struct((4 * CH, CELLS), F32)],
        pair,
        pair_mask,
        in_gain,
        in_bias,
        in_proj,
        scratch=[pltpu.VMEM((2 * CELLS, CH), F32)],
    )
    factors = exchange(factors)
    d_out_proj, d_xnorm, slope = call(
        gate_kernel,
        [struct((CH, CELLS), BF16), wide, wide],
        grad_out,
        normed,
        w_gate,
        w_out,
        flops=500_000_000,
    )
    theirs = swap_cores(factors)
    x_send, left, right = call(
        product_kernel,
        [one, struct((16 * T, 2 * CH), BF16), struct((16 * T, 2 * CH), BF16)],
        parity,
        factors.reshape(8, 2, 8, 2 * SUB, CH),
        theirs.reshape(8, 2, 8, 2 * SUB, CH),
        smem=(0,),
    )
    x_recv = exchange(x_send)
    dx_send, xhat = call(
        inner_kernel,
        [one, wide],
        x_recv,
        d_xnorm,
        x_gain,
        scratch=[pltpu.VMEM((CELLS, CH), F32)],
    )
    dx = exchange(dx_send)
    g_gate, g_out, inner, partial = call(
        output_kernel,
        [square, square, square, wide],
        xhat,
        d_xnorm,
        slope,
        d_out_proj,
        normed,
        x_gain,
        x_bias,
        w_out,
        w_gate,
        flops=500_000_000,
    )
    (back_send,) = call(back_kernel, [two], parity, dx, swap_cores(dx), left, right, smem=(0,))
    back = exchange(back_send)
    weights, d_normed = call(
        project_kernel,
        [struct((CH, SUB, CH), F32), wide],
        back,
        coef,
        normed,
        zhat,
        partial,
        in_proj,
        g_gate,
        g_out,
        inner,
        scratch=[pltpu.VMEM((2 * CELLS, CH), F32), pltpu.VMEM((CELLS, CH), F32)],
    )
    weights = exchange(weights)
    (grad_pair,) = call(
        pair_kernel,
        [struct((T, T, CH), BF16)],
        d_normed,
        zhat,
        zinv,
        in_gain,
        flops=500_000_000,
    )
    (totals,) = call(total_kernel, [struct((CH, SUB, CH), F32)], weights)
    totals = exchange(totals)
    g_in, g_gate, g_out, ln_in, inner = call(
        unpack_kernel,
        [struct((CH, 4 * CH), F32), square, square, struct((2, CH), F32), struct((2, CH), F32)],
        totals,
        swap_cores(totals),
        scratch=[pltpu.VMEM((CELLS, CH), F32)],
    )
    return grad_pair, g_in, g_gate, g_out, ln_in, inner


def solution(mesh):
    cells = P("row", ("col", "depth"), None)
    return jax.shard_map(
        per_device,
        mesh=mesh,
        in_specs=(cells, cells, P("row", ("col", "depth"))) + (P(),) * 7,
        out_specs=(cells,) + (P(),) * 5,
        check_vma=False,
    )
```

```python
import jax
import jax.numpy as jnp
from jax import lax
from jax.experimental import pallas as pl
from jax.experimental.pallas import tpu as pltpu
from jax.sharding import PartitionSpec as P

F32 = jnp.float32
BF16 = jnp.bfloat16
PLANE = ("row", "col")
T = 32
CH = 128
CELLS = T * T
SUB = 8
GROUPS = T // SUB
HALF = SUB // 2


def call(kernel, outs, *args, scratch=(), flops=2_000_000, spaces=None, fetched=()):
    spaces = spaces or {}
    fetched = tuple(fetched)
    count = len(args)
    specs = [
        pl.BlockSpec(memory_space=pltpu.HBM if i in fetched else spaces.get(i, pltpu.VMEM))
        for i in range(count)
    ]
    moved = sum(a.size * a.dtype.itemsize for a in args)
    moved += sum(o.size * o.dtype.itemsize for o in outs)
    args = [
        pltpu.with_memory_space_constraint(a, pltpu.HBM) if i in fetched else a
        for i, a in enumerate(args)
    ]

    def body(*refs):
        if not fetched:
            return kernel(*refs)
        local = refs[len(refs) - 1 - len(fetched) : -1]
        refs, sems = refs[: len(refs) - 1 - len(fetched)], refs[-1]
        inputs = list(refs[:count])
        copies = [
            pltpu.make_async_copy(inputs[i], target, sems.at[place])
            for place, (i, target) in enumerate(zip(fetched, local))
        ]
        for copy in copies:
            copy.start()
        for copy in copies:
            copy.wait()
        for i, target in zip(fetched, local):
            inputs[i] = target
        return kernel(*inputs, *refs[count:])

    extra = [pltpu.VMEM(args[i].shape, args[i].dtype) for i in fetched]
    if fetched:
        extra.append(pltpu.SemaphoreType.DMA((len(fetched),)))
    return pl.pallas_call(
        body,
        out_shape=outs,
        in_specs=specs,
        out_specs=[pl.BlockSpec(memory_space=pltpu.VMEM) for _ in outs],
        scratch_shapes=list(scratch) + extra,
        compiler_params=pltpu.CompilerParams(vmem_limit_bytes=32 * 1024 * 1024),
        cost_estimate=pl.CostEstimate(flops=flops, bytes_accessed=moved, transcendentals=0),
    )(*args)


def struct(shape, dtype):
    return jax.ShapeDtypeStruct(shape, dtype)


def column(row):
    return jnp.transpose(jnp.broadcast_to(row, (CH, CH)))[:, :1]


def dot(a, b, ca, cb):
    return lax.dot_general(a, b, (((ca,), (cb,)), ((), ())), preferred_element_type=F32)


def channel_major(ref):
    chunks = []
    for s in range(SUB):
        block = jnp.concatenate([ref[SUB * g + s] for g in range(GROUPS)], axis=0)
        chunks.append(jnp.transpose(block.astype(F32)))
    return jnp.concatenate(chunks, axis=1)


def to_tiles(value, scratch, first, stride):
    for s in range(SUB):
        scratch[pl.ds(first + s, CH, stride=stride), :] = value[:, s * CH : (s + 1) * CH]


def from_tiles(scratch, first, stride):
    return jnp.concatenate(
        [scratch[pl.ds(first + s, CH, stride=stride), :] for s in range(SUB)], axis=1
    )


def norm(value):
    centre = value - jnp.mean(value, axis=0, keepdims=True)
    inverse = lax.rsqrt(jnp.mean(centre * centre, axis=0, keepdims=True) + 1e-05)
    return centre * inverse, inverse


def norm_back(tangent, scaled, inverse):
    first = jnp.mean(tangent, axis=0, keepdims=True)
    second = jnp.mean(tangent * scaled, axis=0, keepdims=True)
    return inverse * (tangent - first - scaled * second)


def swap_groups(parts):
    a, b, c, d = parts
    axis = a.ndim - 1
    lane = lax.broadcasted_iota(jnp.int32, a.shape, axis)
    low = lane < 64
    even = (lane & 32) == 0
    a, c = jnp.where(low, a, pltpu.roll(c, 64, axis)), jnp.where(low, pltpu.roll(a, 64, axis), c)
    b, d = jnp.where(low, b, pltpu.roll(d, 64, axis)), jnp.where(low, pltpu.roll(b, 64, axis), d)
    a, b = jnp.where(even, a, pltpu.roll(b, 32, axis)), jnp.where(even, pltpu.roll(a, 96, axis), b)
    c, d = jnp.where(even, c, pltpu.roll(d, 32, axis)), jnp.where(even, pltpu.roll(c, 96, axis), d)
    return a, b, c, d


def to_matrix(tiles):
    blocks = tiles.shape[0]
    halves = []
    for half in range(2):
        parts = [tiles[:, half * 4 + part].astype(F32) for part in range(4)]
        rows = jnp.stack(swap_groups(parts), axis=1)
        halves.append(rows.reshape(blocks * T, CH))
    return jnp.concatenate(halves, axis=1)


def from_matrix(matrix):
    blocks = matrix.shape[0] // T
    parts = []
    for half in range(2):
        rows = matrix[:, half * CH : (half + 1) * CH].reshape(blocks, GROUPS, SUB, CH)
        parts += list(swap_groups([rows[:, g] for g in range(GROUPS)]))
    return jnp.stack(parts, axis=1)


def normalise(pair, gain, bias):
    scaled, inverse = norm(channel_major(pair))
    return scaled, inverse, (scaled * column(gain[...]) + column(bias[...])).astype(BF16)


def factors_of(normed, mask, in_proj):
    proj = dot(in_proj[...], normed, 0, 0)
    flags = mask[...].astype(F32)
    tile = jnp.concatenate([flags[SUB * g : SUB * (g + 1)] for g in range(GROUPS)], axis=1)
    m = jnp.concatenate([tile[s : s + 1] for s in range(SUB)], axis=1)
    sides = []
    for side in range(2):
        val = proj[2 * side * CH : (2 * side + 1) * CH]
        sig = jax.nn.sigmoid(proj[(2 * side + 1) * CH : (2 * side + 2) * CH])
        gated = sig * m
        sides.append((gated, gated * val, 1.0 - sig))
    return sides


def factors_kernel(pair, mask, gain, bias, in_proj, send, scratch):
    normed = normalise(pair, gain, bias)[2]
    for side, (_, factor, _) in enumerate(factors_of(normed, mask, in_proj)):
        to_tiles(factor, scratch, side * SUB, 2 * SUB)
    send[...] = scratch[...].reshape(CH, 2 * SUB, CH).astype(BF16)


def gated_grad(grad_out, normed, w_gate):
    gate = jax.nn.sigmoid(dot(w_gate[...], normed, 0, 0))
    moved = channel_major(grad_out) * gate
    return moved.astype(BF16), moved * (1.0 - gate)


def tangent_kernel(pair, grad_out, gain, bias, x_gain, w_gate, w_out, tangent):
    normed = normalise(pair, gain, bias)[2]
    d_out_proj, _ = gated_grad(grad_out, normed, w_gate)
    tangent[...] = dot(w_out[...], d_out_proj, 1, 0) * column(x_gain[...])


def product_rows(tiles, mine):
    return to_matrix(tiles[:, pl.ds(mine, 1), :, SUB:].reshape(8, 8, SUB, CH)).astype(BF16)


def product_own_kernel(parity, own, left_out, right_out, partial):
    mine = lax.bitwise_and(parity[0], 1)
    left = to_matrix(own[:, :, :, :SUB].reshape(16, 8, SUB, CH)).astype(BF16)
    left_out[...] = left
    right_out[...] = to_matrix(own[:, :, :, SUB:].reshape(16, 8, SUB, CH)).astype(BF16)
    partial[...] = dot(left, product_rows(own, mine), 1, 1)


def product_kernel(parity, other, partial, send):
    mine = lax.bitwise_and(parity[0], 1)
    left = to_matrix(other[:, :, :, :SUB].reshape(16, 8, SUB, CH)).astype(BF16)
    x = partial[...] + dot(left, product_rows(other, mine), 1, 1)
    send[...] = from_matrix(x).reshape(CH, SUB, CH).astype(BF16)


def inner_kernel(recv, tangent, send, scratch):
    scratch[...] = recv[...].astype(F32).reshape(CELLS, CH)
    scaled, inverse = norm(from_tiles(scratch, 0, SUB))
    to_tiles(norm_back(tangent[...], scaled, inverse), scratch, 0, SUB)
    send[...] = scratch[...].reshape(CH, SUB, CH).astype(BF16)


def sums(first, second, place):
    lane = lax.broadcasted_iota(jnp.int32, (CH, CH), 1)
    a = jnp.sum(first, axis=1, keepdims=True)
    b = jnp.sum(second, axis=1, keepdims=True)
    return jnp.where(lane == place, a, jnp.where(lane == place + 1, b, 0.0))


def output_kernel(
    pair,
    grad_out,
    mask,
    gain,
    bias,
    x_gain,
    x_bias,
    in_proj,
    w_gate,
    w_out,
    x_recv,
    after,
    coef,
    normed_out,
    zhat,
    partial,
    early,
    scratch,
):
    scaled, _, normed = normalise(pair, gain, bias)
    zhat[...] = scaled.astype(BF16)
    normed_out[...] = normed
    for side, (gated, factor, rest) in enumerate(factors_of(normed, mask, in_proj)):
        coef[2 * side * CH : (2 * side + 1) * CH] = gated.astype(BF16)
        coef[(2 * side + 1) * CH : (2 * side + 2) * CH] = (factor * rest).astype(BF16)
    d_out_proj, slope = gated_grad(grad_out, normed, w_gate)
    d_xnorm = dot(w_out[...], d_out_proj, 1, 0)
    scratch[...] = x_recv[...].astype(F32).reshape(CELLS, CH)
    xhat, _ = norm(from_tiles(scratch, 0, SUB))
    xnorm = (xhat * column(x_gain[...]) + column(x_bias[...])).astype(BF16)
    d_gate_pre = (slope * dot(w_out[...], xnorm, 0, 0)).astype(BF16)
    early[0:CH] = dot(normed, d_gate_pre, 1, 1)
    early[CH : 2 * CH] = dot(xnorm, d_out_proj, 1, 1)
    early[2 * CH :] = sums(d_xnorm * xhat, d_xnorm, 2)
    partial[...] = dot(w_gate[...], d_gate_pre, 1, 0)


def back_kernel(dx, left, right, send):
    pairs = right[...].reshape(8, 2, T, 2 * CH)
    da = None
    dbs = []
    for half in range(2):
        grad = to_matrix(dx[half].reshape(16, 8, SUB, CH)).astype(BF16)
        term = dot(grad, pairs[:, half].reshape(8 * T, 2 * CH), 1, 0)
        da = term if da is None else da + term
        dbs.append(dot(grad, left[...], 0, 0).reshape(8, T, 2 * CH))
    db = jnp.stack(dbs, axis=1).reshape(16 * T, 2 * CH)
    send[:, :SUB] = from_matrix(da).reshape(CH, SUB, CH).astype(BF16)
    send[:, SUB:] = from_matrix(db).reshape(CH, SUB, CH).astype(BF16)


def project_kernel(recv, in_proj, coef, normed, zhat, partial, early, send, d_normed, scratch, packed):
    scratch[...] = recv[...].astype(F32).reshape(2 * CELLS, CH)
    da = from_tiles(scratch, 0, 2 * SUB)
    db = from_tiles(scratch, SUB, 2 * SUB)
    d_proj = jnp.concatenate(
        [
            (grad * coef[part * CH : (part + 1) * CH].astype(F32)).astype(BF16)
            for part, grad in enumerate((da, da, db, db))
        ],
        axis=0,
    )
    g_in = dot(normed[...], d_proj, 1, 1)
    grad = dot(in_proj[...], d_proj, 1, 0) + partial[...]
    d_normed[...] = grad
    for part in range(4):
        packed[pl.ds(part, CH, stride=SUB), :] = g_in[:, part * CH : (part + 1) * CH]
    packed[pl.ds(4, CH, stride=SUB), :] = early[0:CH]
    packed[pl.ds(5, CH, stride=SUB), :] = early[CH : 2 * CH]
    packed[pl.ds(6, CH, stride=SUB), :] = early[2 * CH :] + sums(
        grad * zhat[...].astype(F32), grad, 0
    )
    packed[pl.ds(7, CH, stride=SUB), :] = jnp.zeros((CH, CH), F32)
    send[...] = packed[...].reshape(CH, SUB, CH).astype(BF16)


def pair_kernel(d_normed, pair, gain, out):
    scaled, inverse = norm(channel_major(pair))
    grad = norm_back(d_normed[...] * column(gain[...]), scaled, inverse)
    for s in range(SUB):
        block = jnp.transpose(grad[:, s * CH : (s + 1) * CH]).astype(BF16)
        for g in range(GROUPS):
            out[SUB * g + s] = block[g * T : (g + 1) * T]


def total_kernel(recv, after, send):
    total = jnp.sum(recv[...].astype(F32), axis=0, keepdims=True)
    total = total + pltpu.roll(total, HALF, 1)
    send[...] = jnp.broadcast_to(total, (CH // 2, SUB, CH)).astype(BF16)


def unpack_kernel(totals, g_in, g_gate, g_out, ln_in, inner, scratch):
    scratch[...] = totals[...].astype(F32).reshape(CELLS, CH)
    for part in range(HALF):
        g_in[:, part * CH : (part + 1) * CH] = scratch[pl.ds(part, CH, stride=HALF), :]
    g_gate[...] = scratch[pl.ds(CELLS // 2, CH, stride=HALF), :]
    g_out[...] = scratch[pl.ds(CELLS // 2 + 1, CH, stride=HALF), :]
    norms = jnp.transpose(scratch[pl.ds(CELLS // 2 + 2, CH, stride=HALF), :])
    ln_in[...] = norms[0:2]
    inner[...] = norms[2:4]


def swap_cores(value):
    return lax.ppermute(value, "depth", [(0, 1), (1, 0)])


def both_cores(value):
    return lax.all_gather(value, "depth", axis=0, tiled=False)


def exchange(value, axes=PLANE):
    return lax.all_to_all(value, axes, 0, 0, tiled=True)


def per_device(
    pair,
    grad_out,
    pair_mask,
    ln_in_gain,
    ln_in_bias,
    in_proj,
    w_gate,
    inner_norm_gain,
    inner_norm_bias,
    w_out,
):
    parity = lax.axis_index("depth").astype(jnp.int32).reshape(1)
    in_gain = ln_in_gain.reshape(1, CH)
    in_bias = ln_in_bias.reshape(1, CH)
    x_gain = inner_norm_gain.reshape(1, CH)
    x_bias = inner_norm_bias.reshape(1, CH)
    one = struct((CH, SUB, CH), BF16)
    two = struct((CH, 2 * SUB, CH), BF16)
    square = struct((CH, CH), F32)
    matrix = struct((16 * T, 2 * CH), BF16)
    wide = struct((CH, CELLS), F32)
    narrow = struct((CH, CELLS), BF16)
    tiles = pltpu.VMEM((CELLS, CH), F32)
    pairs_of_tiles = pltpu.VMEM((2 * CELLS, CH), F32)

    (factors,) = call(
        factors_kernel,
        [two],
        pair,
        pair_mask,
        in_gain,
        in_bias,
        in_proj,
        scratch=[pairs_of_tiles],
        fetched=range(5),
    )
    factors = exchange(factors).reshape(8, 2, 8, 2 * SUB, CH)
    left, right, partial = call(
        product_own_kernel,
        [matrix, matrix, struct((16 * T, 2 * CH), F32)],
        parity,
        factors,
        spaces={0: pltpu.SMEM},
    )
    (x_send,) = call(
        product_kernel, [one], parity, swap_cores(factors), partial, spaces={0: pltpu.SMEM}
    )
    x_recv = exchange(x_send)
    (tangent,) = call(
        tangent_kernel,
        [wide],
        pair,
        grad_out,
        in_gain,
        in_bias,
        x_gain,
        w_gate,
        w_out,
        flops=500_000_000,
        fetched=range(7),
    )
    (dx_send,) = call(inner_kernel, [one], x_recv, tangent, scratch=[tiles])
    (back_send,) = call(back_kernel, [two], both_cores(exchange(dx_send)), left, right)
    back = exchange(back_send)
    coef, normed, zhat, partial, early = call(
        output_kernel,
        [struct((4 * CH, CELLS), BF16), narrow, narrow, wide, struct((3 * CH, CH), F32)],
        pair,
        grad_out,
        pair_mask,
        in_gain,
        in_bias,
        x_gain,
        x_bias,
        in_proj,
        w_gate,
        w_out,
        x_recv,
        back_send,
        scratch=[tiles],
        flops=500_000_000,
        fetched=range(10),
        spaces={11: pl.ANY},
    )
    weights, d_normed = call(
        project_kernel,
        [one, wide],
        back,
        in_proj,
        coef,
        normed,
        zhat,
        partial,
        early,
        scratch=[pairs_of_tiles, tiles],
    )
    weights = exchange(weights.reshape(2 * CH, HALF, CH), ("row", "col", "depth"))
    (grad_pair,) = call(
        pair_kernel,
        [struct((T, T, CH), BF16)],
        d_normed,
        pair,
        in_gain,
        flops=500_000_000,
        fetched=(1, 2),
    )
    (totals,) = call(
        total_kernel,
        [struct((CH // 2, SUB, CH), BF16)],
        weights.reshape(CH, SUB, CH),
        grad_pair,
        spaces={1: pl.ANY},
    )
    totals = exchange(totals.reshape(CH, HALF, CH))
    g_in, g_gate, g_out, ln_in, inner = call(
        unpack_kernel,
        [struct((CH, 4 * CH), F32), square, square, struct((2, CH), F32), struct((2, CH), F32)],
        both_cores(totals.reshape(CH // 2, SUB, CH)),
        scratch=[tiles],
    )
    return grad_pair, g_in, g_gate, g_out, ln_in, inner


def solution(mesh):
    cells = P("row", ("col", "depth"), None)
    return jax.shard_map(
        per_device,
        mesh=mesh,
        in_specs=(cells, cells, P("row", ("col", "depth"))) + (P(),) * 7,
        out_specs=(cells,) + (P(),) * 5,
        check_vma=False,
    )
```

```python
import jax
import jax.numpy as jnp
from jax import lax
from jax.experimental import pallas as pl
from jax.experimental.pallas import tpu as pltpu
from jax.sharding import Mesh
from jax.sharding import PartitionSpec as P

F32 = jnp.float32
BF16 = jnp.bfloat16
T = 32
CH = 128
CELLS = T * T
SUB = 8
GROUPS = T // SUB
ROW = ("y", "z_lo")
COL = ("x", "z_hi")
SIZES = (4, 4, 4, 2, 2)
PLANE = ("z_lo", "y") + COL
FLAT = ("depth", "y", "x")
UPRIGHT = ("z_lo", "z_hi")
PARTS = 32
PEERS = 8
PART = CELLS // PARTS


def call(kernel, outs, *args, scratch=(), flops=2_000_000, spaces=None, fetched=(), hbm=(), hbm_outs=()):
    spaces = spaces or {}
    fetched = tuple(fetched)
    hbm = fetched + tuple(hbm)
    count = len(args)
    specs = [
        pl.BlockSpec(memory_space=pltpu.HBM if i in hbm else spaces.get(i, pltpu.VMEM))
        for i in range(count)
    ]
    moved = sum(a.size * a.dtype.itemsize for a in args)
    moved += sum(o.size * o.dtype.itemsize for o in outs)
    args = [
        pltpu.with_memory_space_constraint(a, pltpu.HBM) if i in hbm else a
        for i, a in enumerate(args)
    ]

    def body(*refs):
        if not fetched:
            return kernel(*refs)
        local = refs[len(refs) - 1 - len(fetched) : -1]
        refs, sems = refs[: len(refs) - 1 - len(fetched)], refs[-1]
        inputs = list(refs[:count])
        copies = [
            pltpu.make_async_copy(inputs[i], target, sems.at[place])
            for place, (i, target) in enumerate(zip(fetched, local))
        ]
        for copy in copies:
            copy.start()
        for copy in copies:
            copy.wait()
        for i, target in zip(fetched, local):
            inputs[i] = target
        return kernel(*inputs, *refs[count:])

    extra = [pltpu.VMEM(args[i].shape, args[i].dtype) for i in fetched]
    if fetched:
        extra.append(pltpu.SemaphoreType.DMA((len(fetched),)))
    return pl.pallas_call(
        body,
        out_shape=[pltpu.HBM(o.shape, o.dtype) if i in hbm_outs else o for i, o in enumerate(outs)],
        in_specs=specs,
        out_specs=[
            pl.BlockSpec(memory_space=pltpu.HBM if i in hbm_outs else pltpu.VMEM)
            for i in range(len(outs))
        ],
        scratch_shapes=list(scratch) + extra,
        compiler_params=pltpu.CompilerParams(vmem_limit_bytes=32 * 1024 * 1024),
        cost_estimate=pl.CostEstimate(flops=flops, bytes_accessed=moved, transcendentals=0),
    )(*args)


def struct(shape, dtype):
    return jax.ShapeDtypeStruct(shape, dtype)


def column(row):
    return jnp.transpose(jnp.broadcast_to(row, (CH, CH)))[:, :1]


def dot(a, b, ca, cb):
    return lax.dot_general(a, b, (((ca,), (cb,)), ((), ())), preferred_element_type=F32)


def channel_major(ref):
    chunks = []
    for s in range(SUB):
        block = jnp.concatenate([ref[SUB * g + s] for g in range(GROUPS)], axis=0)
        chunks.append(jnp.transpose(block.astype(F32)))
    return jnp.concatenate(chunks, axis=1)


def to_tiles(value, scratch, first, stride):
    for s in range(SUB):
        scratch[pl.ds(first + s, CH, stride=stride), :] = value[:, s * CH : (s + 1) * CH]


def from_tiles(scratch, first, stride):
    return jnp.concatenate(
        [scratch[pl.ds(first + s, CH, stride=stride), :] for s in range(SUB)], axis=1
    )


def norm(value):
    centre = value - jnp.mean(value, axis=0, keepdims=True)
    inverse = lax.rsqrt(jnp.mean(centre * centre, axis=0, keepdims=True) + 1e-05)
    return centre * inverse, inverse


def norm_back(tangent, scaled, inverse):
    first = jnp.mean(tangent, axis=0, keepdims=True)
    second = jnp.mean(tangent * scaled, axis=0, keepdims=True)
    return inverse * (tangent - first - scaled * second)


def swap_groups(parts):
    a, b, c, d = parts
    axis = a.ndim - 1
    lane = lax.broadcasted_iota(jnp.int32, a.shape, axis)
    low = lane < 64
    even = (lane & 32) == 0
    a, c = jnp.where(low, a, pltpu.roll(c, 64, axis)), jnp.where(low, pltpu.roll(a, 64, axis), c)
    b, d = jnp.where(low, b, pltpu.roll(d, 64, axis)), jnp.where(low, pltpu.roll(b, 64, axis), d)
    a, b = jnp.where(even, a, pltpu.roll(b, 32, axis)), jnp.where(even, pltpu.roll(a, 96, axis), b)
    c, d = jnp.where(even, c, pltpu.roll(d, 32, axis)), jnp.where(even, pltpu.roll(c, 96, axis), d)
    return a, b, c, d


def to_matrix(tiles):
    blocks = tiles.shape[0]
    halves = []
    for half in range(2):
        parts = [tiles[:, 2 * part + half].astype(F32) for part in range(4)]
        rows = jnp.stack(swap_groups(parts), axis=1)
        halves.append(rows.reshape(blocks * T, CH))
    return jnp.concatenate(halves, axis=1)


def from_matrix(matrix):
    blocks = matrix.shape[0] // T
    halves = []
    for half in range(2):
        rows = matrix[:, half * CH : (half + 1) * CH].reshape(blocks, GROUPS, SUB, CH)
        halves.append(swap_groups([rows[:, g] for g in range(GROUPS)]))
    return jnp.stack([halves[half][part] for part in range(4) for half in range(2)], axis=1)


def normalise(pair, gain, bias):
    scaled, inverse = norm(channel_major(pair))
    return scaled, inverse, (scaled * column(gain[...]) + column(bias[...])).astype(BF16)


def factors_of(normed, mask, in_proj):
    proj = dot(in_proj[...], normed, 0, 0)
    flags = mask[...].astype(F32)
    tile = jnp.concatenate([flags[SUB * g : SUB * (g + 1)] for g in range(GROUPS)], axis=1)
    m = jnp.concatenate([tile[s : s + 1] for s in range(SUB)], axis=1)
    sides = []
    for side in range(2):
        val = proj[2 * side * CH : (2 * side + 1) * CH]
        sig = jax.nn.sigmoid(proj[(2 * side + 1) * CH : (2 * side + 2) * CH])
        gated = sig * m
        sides.append((gated, gated * val, 1.0 - sig))
    return sides


def factors_kernel(pair, mask, gain, bias, in_proj, send, scratch):
    normed = normalise(pair, gain, bias)[2]
    for side, (_, factor, _) in enumerate(factors_of(normed, mask, in_proj)):
        to_tiles(factor, scratch, side * SUB, 2 * SUB)
    send[...] = scratch[...].reshape(CH, 2 * SUB, CH).astype(BF16)


def gated_grad(grad_out, normed, w_gate):
    gate = jax.nn.sigmoid(dot(w_gate[...], normed, 0, 0))
    moved = channel_major(grad_out) * gate
    return moved.astype(BF16), moved * (1.0 - gate)


def tangent_kernel(pair, grad_out, gain, bias, x_gain, w_gate, w_out, tangent):
    normed = normalise(pair, gain, bias)[2]
    d_out_proj, _ = gated_grad(grad_out, normed, w_gate)
    tangent[...] = dot(w_out[...], d_out_proj, 1, 0) * column(x_gain[...])


def product_theirs_kernel(parity, own, left_out, theirs):
    other = 1 - lax.bitwise_and(parity[0], 1)
    left = to_matrix(own[:, :, :, :, :SUB].reshape(16, 8, SUB, CH)).astype(BF16)
    left_out[...] = left
    right = to_matrix(own[:, pl.ds(other, 1), :, :, SUB:].reshape(8, 8, SUB, CH)).astype(BF16)
    theirs[...] = from_matrix(dot(left, right, 1, 1)).reshape(CH, SUB, CH).astype(BF16)


def product_mine_kernel(parity, own, left, right_out, mine):
    place = lax.bitwise_and(parity[0], 1)
    right_out[...] = to_matrix(own[:, :, :, :, SUB:].reshape(16, 8, SUB, CH)).astype(BF16)
    right = to_matrix(own[:, pl.ds(place, 1), :, :, SUB:].reshape(8, 8, SUB, CH)).astype(BF16)
    mine[...] = from_matrix(dot(left[...], right, 1, 1)).reshape(CH, SUB, CH)


def product_kernel(mine, got, send):
    send[...] = (mine[...] + got[...].astype(F32)).astype(BF16)


def inner_kernel(recv, tangent, send, scratch):
    scratch[...] = recv[...].astype(F32).reshape(CELLS, CH)
    scaled, inverse = norm(from_tiles(scratch, 0, SUB))
    to_tiles(norm_back(tangent[...], scaled, inverse), scratch, 0, SUB)
    send[...] = scratch[...].reshape(CH, SUB, CH).astype(BF16)


def sums(first, second, place):
    lane = lax.broadcasted_iota(jnp.int32, (CH, CH), 1)
    a = jnp.sum(first, axis=1, keepdims=True)
    b = jnp.sum(second, axis=1, keepdims=True)
    return jnp.where(lane == place, a, jnp.where(lane == place + 1, b, 0.0))


def output_kernel(
    pair,
    grad_out,
    mask,
    gain,
    bias,
    x_gain,
    x_bias,
    in_proj,
    w_gate,
    w_out,
    x_recv,
    after,
    coef,
    normed_out,
    zhat,
    partial,
    early,
    scratch,
):
    scaled, _, normed = normalise(pair, gain, bias)
    zhat[...] = scaled.astype(BF16)
    normed_out[...] = normed
    for side, (gated, factor, rest) in enumerate(factors_of(normed, mask, in_proj)):
        coef[2 * side * CH : (2 * side + 1) * CH] = gated.astype(BF16)
        coef[(2 * side + 1) * CH : (2 * side + 2) * CH] = (factor * rest).astype(BF16)
    d_out_proj, slope = gated_grad(grad_out, normed, w_gate)
    d_xnorm = dot(w_out[...], d_out_proj, 1, 0)
    scratch[...] = x_recv[...].astype(F32).reshape(CELLS, CH)
    xhat, _ = norm(from_tiles(scratch, 0, SUB))
    xnorm = (xhat * column(x_gain[...]) + column(x_bias[...])).astype(BF16)
    d_gate_pre = (slope * dot(w_out[...], xnorm, 0, 0)).astype(BF16)
    early[0:CH] = dot(normed, d_gate_pre, 1, 1)
    early[CH : 2 * CH] = dot(xnorm, d_out_proj, 1, 1)
    early[2 * CH :] = sums(d_xnorm * xhat, d_xnorm, 2)
    partial[...] = dot(w_gate[...], d_gate_pre, 1, 0)


def back_mine_kernel(parity, own, left, right, da, db):
    place = lax.bitwise_and(parity[0], 1)
    grad = to_matrix(own[...].reshape(16, 8, SUB, CH)).astype(BF16)
    da[...] = dot(grad, right[:, pl.ds(place, 1)].reshape(8 * T, 2 * CH), 1, 0)
    db[...] = from_matrix(dot(grad, left[...], 0, 0)).astype(BF16)


def back_kernel(parity, other, left, right, da_mine, db_mine, send):
    place = lax.bitwise_and(parity[0], 1)
    grad = to_matrix(other[...].reshape(16, 8, SUB, CH)).astype(BF16)
    da = da_mine[...] + dot(grad, right[:, pl.ds(1 - place, 1)].reshape(8 * T, 2 * CH), 1, 0)
    db = from_matrix(dot(grad, left[...], 0, 0)).astype(BF16)
    send[:, :, :, :, :SUB] = from_matrix(da).reshape(2, 2, 4, 8, SUB, CH).astype(BF16)
    send[:, pl.ds(place, 1), :, :, SUB:] = db_mine[...].reshape(2, 1, 4, 8, SUB, CH)
    send[:, pl.ds(1 - place, 1), :, :, SUB:] = db.reshape(2, 1, 4, 8, SUB, CH)


def project_kernel(
    recv, in_proj, coef, normed, zhat, partial, early, send, d_normed, scratch, packed, kept, sem
):
    scratch[...] = recv[...].astype(F32).reshape(2 * CELLS, CH)
    da = from_tiles(scratch, 0, 2 * SUB)
    db = from_tiles(scratch, SUB, 2 * SUB)
    d_proj = jnp.concatenate(
        [
            (grad * coef[part * CH : (part + 1) * CH].astype(F32)).astype(BF16)
            for part, grad in enumerate((da, da, db, db))
        ],
        axis=0,
    )
    g_in = dot(normed[...], d_proj, 1, 1)
    grad = dot(in_proj[...], d_proj, 1, 0) + partial[...]
    kept[...] = grad
    copy = pltpu.make_async_copy(kept, d_normed, sem)
    copy.start()
    for part in range(4):
        packed[pl.ds(part, CH, stride=SUB), :] = g_in[:, part * CH : (part + 1) * CH]
    packed[pl.ds(4, CH, stride=SUB), :] = early[0:CH]
    packed[pl.ds(5, CH, stride=SUB), :] = early[CH : 2 * CH]
    packed[pl.ds(6, CH, stride=SUB), :] = early[2 * CH :] + sums(
        grad * zhat[...].astype(F32), grad, 0
    )
    packed[pl.ds(7, CH, stride=SUB), :] = jnp.zeros((CH, CH), F32)
    send[...] = packed[...].reshape(CH, SUB, CH).astype(BF16)
    copy.wait()


def pair_kernel(d_normed, pair, gain, out):
    scaled, inverse = norm(channel_major(pair))
    grad = norm_back(d_normed[...] * column(gain[...]), scaled, inverse)
    for s in range(SUB):
        block = jnp.transpose(grad[:, s * CH : (s + 1) * CH]).astype(BF16)
        for g in range(GROUPS):
            out[SUB * g + s] = block[g * T : (g + 1) * T]


def total_kernel(recv, after, send):
    total = jnp.sum(recv[...].astype(F32), axis=0, keepdims=True)
    send[...] = jnp.broadcast_to(total, send.shape).astype(BF16)


def unpack_kernel(totals, g_in, g_gate, g_out, ln_in, inner, scratch):
    scratch[...] = totals[...].astype(F32).reshape(CELLS, CH)
    for part in range(4):
        g_in[:, part * CH : (part + 1) * CH] = scratch[pl.ds(part, CH, stride=SUB), :]
    g_gate[...] = scratch[pl.ds(4, CH, stride=SUB), :]
    g_out[...] = scratch[pl.ds(5, CH, stride=SUB), :]
    norms = jnp.transpose(scratch[pl.ds(6, CH, stride=SUB), :])
    ln_in[...] = norms[0:2]
    inner[...] = norms[2:4]


def swap_cores(value):
    return lax.ppermute(value, "depth", [(0, 1), (1, 0)])


def exchange(value, axes=PLANE):
    return lax.all_to_all(value, axes, 0, 0, tiled=True)


def per_device(
    pair,
    grad_out,
    pair_mask,
    ln_in_gain,
    ln_in_bias,
    in_proj,
    w_gate,
    inner_norm_gain,
    inner_norm_bias,
    w_out,
):
    parity = lax.axis_index("depth").astype(jnp.int32).reshape(1)
    in_gain = ln_in_gain.reshape(1, CH)
    in_bias = ln_in_bias.reshape(1, CH)
    x_gain = inner_norm_gain.reshape(1, CH)
    x_bias = inner_norm_bias.reshape(1, CH)
    one = struct((CH, SUB, CH), BF16)
    two = struct((CH, 2 * SUB, CH), BF16)
    square = struct((CH, CH), F32)
    matrix = struct((16 * T, 2 * CH), BF16)
    wide = struct((CH, CELLS), F32)
    narrow = struct((CH, CELLS), BF16)
    tiles = pltpu.VMEM((CELLS, CH), F32)
    pairs_of_tiles = pltpu.VMEM((2 * CELLS, CH), F32)

    (factors,) = call(
        factors_kernel,
        [two],
        pair,
        pair_mask,
        in_gain,
        in_bias,
        in_proj,
        scratch=[pairs_of_tiles],
        fetched=range(5),
    )
    factors, parity = lax.optimization_barrier((factors, parity))
    factors = exchange(factors).reshape(2, 2, 4, 8, 2 * SUB, CH)
    left, x_theirs = call(
        product_theirs_kernel, [matrix, one], parity, factors, spaces={0: pltpu.SMEM}
    )
    x_got = swap_cores(x_theirs)
    right, x_mine = call(
        product_mine_kernel,
        [matrix, struct((CH, SUB, CH), F32)],
        parity,
        factors,
        left,
        spaces={0: pltpu.SMEM},
    )
    right = right.reshape(2, 2, 4 * T, 2 * CH)
    (x_send,) = call(product_kernel, [one], x_mine, x_got)
    x_recv = exchange(x_send)
    (tangent,) = call(
        tangent_kernel,
        [wide],
        pair,
        grad_out,
        in_gain,
        in_bias,
        x_gain,
        w_gate,
        w_out,
        flops=500_000_000,
        fetched=range(7),
    )
    (dx_send,) = call(inner_kernel, [one], x_recv, tangent, scratch=[tiles])
    dx = exchange(dx_send)
    da, db = call(
        back_mine_kernel,
        [struct((16 * T, 2 * CH), F32), struct((8, 8, SUB, CH), BF16)],
        parity,
        dx,
        left,
        right,
        spaces={0: pltpu.SMEM},
    )
    (back_send,) = call(
        back_kernel,
        [struct((2, 2, 4, 8, 2 * SUB, CH), BF16)],
        parity,
        swap_cores(dx),
        left,
        right,
        da,
        db,
        spaces={0: pltpu.SMEM},
    )
    back_send = back_send.reshape(CH, 2 * SUB, CH)
    back = exchange(back_send)
    coef, normed, zhat, partial, early = call(
        output_kernel,
        [struct((4 * CH, CELLS), BF16), narrow, narrow, wide, struct((3 * CH, CH), F32)],
        pair,
        grad_out,
        pair_mask,
        in_gain,
        in_bias,
        x_gain,
        x_bias,
        in_proj,
        w_gate,
        w_out,
        x_recv,
        back_send,
        scratch=[tiles],
        flops=500_000_000,
        fetched=range(10),
        hbm=(11,),
    )
    weights, d_normed = call(
        project_kernel,
        [one, wide],
        back,
        in_proj,
        coef,
        normed,
        zhat,
        partial,
        early,
        scratch=[
            pairs_of_tiles,
            tiles,
            pltpu.VMEM((CH, CELLS), F32),
            pltpu.SemaphoreType.DMA,
        ],
        hbm_outs=(1,),
    )
    weights = exchange(weights.reshape(PARTS, PART, CH), FLAT)
    (grad_pair,) = call(
        pair_kernel,
        [struct((T, T, CH), BF16)],
        d_normed,
        pair,
        in_gain,
        flops=500_000_000,
        fetched=range(3),
    )
    (totals,) = call(
        total_kernel, [struct((PEERS, PART, CH), BF16)], weights, grad_pair, hbm=(1,)
    )
    totals = exchange(totals, UPRIGHT)
    (totals,) = call(
        total_kernel, [struct((PARTS, PART, CH), BF16)], totals, grad_pair, hbm=(1,)
    )
    totals = exchange(totals, FLAT).reshape(CH, SUB, CH)
    g_in, g_gate, g_out, ln_in, inner = call(
        unpack_kernel,
        [struct((CH, 4 * CH), F32), square, square, struct((2, CH), F32), struct((2, CH), F32)],
        totals,
        scratch=[tiles],
    )
    return grad_pair, g_in, g_gate, g_out, ln_in, inner


def solution(mesh):
    fine = Mesh(mesh.devices.reshape(SIZES), ROW + COL + ("depth",))
    cells = P(ROW, COL + ("depth",), None)
    return jax.shard_map(
        per_device,
        mesh=fine,
        in_specs=(cells, cells, P(ROW, COL + ("depth",))) + (P(),) * 7,
        out_specs=(cells,) + (P(),) * 5,
        check_vma=False,
    )
```

```python
import itertools

import jax
import jax.numpy as jnp
from jax import lax
from jax.experimental import pallas as pl
from jax.experimental.pallas import tpu as pltpu
from jax.sharding import Mesh
from jax.sharding import PartitionSpec as P

F32 = jnp.float32
BF16 = jnp.bfloat16
T = 32
CH = 128
CELLS = T * T
SUB = 8
GROUPS = T // SUB
ROW = ("y", "z_lo")
COL = ("x", "z_hi")
SIZES = (4, 4, 4, 2, 2)
AXES = ROW + COL + ("depth",)
ORIGIN = {"z_lo": 2, "y": 3, "x": 3, "z_hi": 1, "depth": 0}
PLANE = ("z_lo", "y", "x", "z_hi")
FLAT = ("depth", "y", "x")
UPRIGHT = ("z_lo", "z_hi")
PARTS = 32
PEERS = 8
PART = CELLS // PARTS


def groups(axes):
    sizes = dict(zip(AXES, SIZES))
    rest = [axis for axis in AXES if axis not in axes]
    listed = []
    for outer in itertools.product(*(range(sizes[axis]) for axis in rest)):
        members = []
        for inner in itertools.product(*(range(sizes[axis]) for axis in axes)):
            place = dict(zip(rest, outer))
            for axis, index in zip(axes, inner):
                place[axis] = (index + ORIGIN[axis]) % sizes[axis]
            member = 0
            for axis in AXES:
                member = member * sizes[axis] + place[axis]
            members.append(member)
        listed.append(members)
    return listed


def call(kernel, outs, *args, scratch=(), flops=2_000_000, spaces=None, fetched=(), hbm=(), hbm_outs=()):
    spaces = spaces or {}
    fetched = tuple(fetched)
    hbm = fetched + tuple(hbm)
    count = len(args)
    specs = [
        pl.BlockSpec(memory_space=pltpu.HBM if i in hbm else spaces.get(i, pltpu.VMEM))
        for i in range(count)
    ]
    moved = sum(a.size * a.dtype.itemsize for a in args)
    moved += sum(o.size * o.dtype.itemsize for o in outs)
    args = [
        pltpu.with_memory_space_constraint(a, pltpu.HBM) if i in hbm else a
        for i, a in enumerate(args)
    ]

    def body(*refs):
        if not fetched:
            return kernel(*refs)
        local = refs[len(refs) - 1 - len(fetched) : -1]
        refs, sems = refs[: len(refs) - 1 - len(fetched)], refs[-1]
        inputs = list(refs[:count])
        copies = [
            pltpu.make_async_copy(inputs[i], target, sems.at[place])
            for place, (i, target) in enumerate(zip(fetched, local))
        ]
        for copy in copies:
            copy.start()
        for copy in copies:
            copy.wait()
        for i, target in zip(fetched, local):
            inputs[i] = target
        return kernel(*inputs, *refs[count:])

    extra = [pltpu.VMEM(args[i].shape, args[i].dtype) for i in fetched]
    if fetched:
        extra.append(pltpu.SemaphoreType.DMA((len(fetched),)))
    return pl.pallas_call(
        body,
        out_shape=[pltpu.HBM(o.shape, o.dtype) if i in hbm_outs else o for i, o in enumerate(outs)],
        in_specs=specs,
        out_specs=[
            pl.BlockSpec(memory_space=pltpu.HBM if i in hbm_outs else pltpu.VMEM)
            for i in range(len(outs))
        ],
        scratch_shapes=list(scratch) + extra,
        compiler_params=pltpu.CompilerParams(vmem_limit_bytes=32 * 1024 * 1024),
        cost_estimate=pl.CostEstimate(flops=flops, bytes_accessed=moved, transcendentals=0),
    )(*args)


def struct(shape, dtype):
    return jax.ShapeDtypeStruct(shape, dtype)


def column(row):
    return jnp.transpose(jnp.broadcast_to(row, (CH, CH)))[:, :1]


def dot(a, b, ca, cb):
    return lax.dot_general(a, b, (((ca,), (cb,)), ((), ())), preferred_element_type=F32)


def channel_major(ref):
    chunks = []
    for s in range(SUB):
        block = jnp.concatenate([ref[SUB * g + s] for g in range(GROUPS)], axis=0)
        chunks.append(jnp.transpose(block.astype(F32)))
    return jnp.concatenate(chunks, axis=1)


def to_tiles(value, scratch, first, stride):
    for s in range(SUB):
        scratch[pl.ds(first + s, CH, stride=stride), :] = value[:, s * CH : (s + 1) * CH]


def from_tiles(scratch, first, stride):
    return jnp.concatenate(
        [scratch[pl.ds(first + s, CH, stride=stride), :] for s in range(SUB)], axis=1
    )


def norm(value):
    centre = value - jnp.mean(value, axis=0, keepdims=True)
    inverse = lax.rsqrt(jnp.mean(centre * centre, axis=0, keepdims=True) + 1e-05)
    return centre * inverse, inverse


def norm_back(tangent, scaled, inverse):
    first = jnp.mean(tangent, axis=0, keepdims=True)
    second = jnp.mean(tangent * scaled, axis=0, keepdims=True)
    return inverse * (tangent - first - scaled * second)


def swap_groups(parts):
    a, b, c, d = parts
    axis = a.ndim - 1
    lane = lax.broadcasted_iota(jnp.int32, a.shape, axis)
    low = lane < 64
    even = (lane & 32) == 0
    a, c = jnp.where(low, a, pltpu.roll(c, 64, axis)), jnp.where(low, pltpu.roll(a, 64, axis), c)
    b, d = jnp.where(low, b, pltpu.roll(d, 64, axis)), jnp.where(low, pltpu.roll(b, 64, axis), d)
    a, b = jnp.where(even, a, pltpu.roll(b, 32, axis)), jnp.where(even, pltpu.roll(a, 96, axis), b)
    c, d = jnp.where(even, c, pltpu.roll(d, 32, axis)), jnp.where(even, pltpu.roll(c, 96, axis), d)
    return a, b, c, d


def to_matrix(tiles):
    blocks = tiles.shape[0]
    halves = []
    for half in range(2):
        parts = [tiles[:, 2 * part + half].astype(F32) for part in range(4)]
        rows = jnp.stack(swap_groups(parts), axis=1)
        halves.append(rows.reshape(blocks * T, CH))
    return jnp.concatenate(halves, axis=1)


def from_matrix(matrix):
    blocks = matrix.shape[0] // T
    halves = []
    for half in range(2):
        rows = matrix[:, half * CH : (half + 1) * CH].reshape(blocks, GROUPS, SUB, CH)
        halves.append(swap_groups([rows[:, g] for g in range(GROUPS)]))
    return jnp.stack([halves[half][part] for part in range(4) for half in range(2)], axis=1)


def normalise(pair, gain, bias):
    scaled, inverse = norm(channel_major(pair))
    return scaled, inverse, (scaled * column(gain[...]) + column(bias[...])).astype(BF16)


def factors_of(normed, mask, in_proj):
    proj = dot(in_proj[...], normed, 0, 0)
    flags = mask[...].astype(F32)
    tile = jnp.concatenate([flags[SUB * g : SUB * (g + 1)] for g in range(GROUPS)], axis=1)
    m = jnp.concatenate([tile[s : s + 1] for s in range(SUB)], axis=1)
    sides = []
    for side in range(2):
        val = proj[2 * side * CH : (2 * side + 1) * CH]
        sig = jax.nn.sigmoid(proj[(2 * side + 1) * CH : (2 * side + 2) * CH])
        gated = sig * m
        sides.append((gated, gated * val, 1.0 - sig))
    return sides


def factors_kernel(pair, mask, gain, bias, in_proj, send, scratch):
    normed = normalise(pair, gain, bias)[2]
    for side, (_, factor, _) in enumerate(factors_of(normed, mask, in_proj)):
        to_tiles(factor, scratch, side * SUB, 2 * SUB)
    send[...] = scratch[...].reshape(CH, 2 * SUB, CH).astype(BF16)


def gated_grad(grad_out, normed, w_gate):
    gate = jax.nn.sigmoid(dot(w_gate[...], normed, 0, 0))
    moved = channel_major(grad_out) * gate
    return moved.astype(BF16), moved * (1.0 - gate)


def tangent_kernel(pair, grad_out, gain, bias, x_gain, w_gate, w_out, tangent):
    normed = normalise(pair, gain, bias)[2]
    d_out_proj, _ = gated_grad(grad_out, normed, w_gate)
    tangent[...] = dot(w_out[...], d_out_proj, 1, 0) * column(x_gain[...])


def product_theirs_kernel(parity, own, left_out, theirs):
    other = 1 - lax.bitwise_and(parity[0], 1)
    left = to_matrix(own[:, :, :, :, :SUB].reshape(16, 8, SUB, CH)).astype(BF16)
    left_out[...] = left
    right = to_matrix(own[:, pl.ds(other, 1), :, :, SUB:].reshape(8, 8, SUB, CH)).astype(BF16)
    theirs[...] = from_matrix(dot(left, right, 1, 1)).reshape(CH, SUB, CH).astype(BF16)


def product_mine_kernel(parity, own, left, right_out, mine):
    place = lax.bitwise_and(parity[0], 1)
    right_out[...] = to_matrix(own[:, :, :, :, SUB:].reshape(16, 8, SUB, CH)).astype(BF16)
    right = to_matrix(own[:, pl.ds(place, 1), :, :, SUB:].reshape(8, 8, SUB, CH)).astype(BF16)
    mine[...] = from_matrix(dot(left[...], right, 1, 1)).reshape(CH, SUB, CH)


def product_kernel(mine, got, send):
    send[...] = (mine[...] + got[...].astype(F32)).astype(BF16)


def inner_kernel(recv, tangent, send, scratch):
    scratch[...] = recv[...].astype(F32).reshape(CELLS, CH)
    scaled, inverse = norm(from_tiles(scratch, 0, SUB))
    to_tiles(norm_back(tangent[...], scaled, inverse), scratch, 0, SUB)
    send[...] = scratch[...].reshape(CH, SUB, CH).astype(BF16)


def sums(first, second, place):
    lane = lax.broadcasted_iota(jnp.int32, (CH, CH), 1)
    a = jnp.sum(first, axis=1, keepdims=True)
    b = jnp.sum(second, axis=1, keepdims=True)
    return jnp.where(lane == place, a, jnp.where(lane == place + 1, b, 0.0))


def output_kernel(
    pair,
    grad_out,
    mask,
    gain,
    bias,
    x_gain,
    x_bias,
    in_proj,
    w_gate,
    w_out,
    x_recv,
    after,
    coef,
    normed_out,
    zhat,
    partial,
    early,
    scratch,
):
    scaled, _, normed = normalise(pair, gain, bias)
    zhat[...] = scaled.astype(BF16)
    normed_out[...] = normed
    for side, (gated, factor, rest) in enumerate(factors_of(normed, mask, in_proj)):
        coef[2 * side * CH : (2 * side + 1) * CH] = gated.astype(BF16)
        coef[(2 * side + 1) * CH : (2 * side + 2) * CH] = (factor * rest).astype(BF16)
    d_out_proj, slope = gated_grad(grad_out, normed, w_gate)
    d_xnorm = dot(w_out[...], d_out_proj, 1, 0)
    scratch[...] = x_recv[...].astype(F32).reshape(CELLS, CH)
    xhat, _ = norm(from_tiles(scratch, 0, SUB))
    xnorm = (xhat * column(x_gain[...]) + column(x_bias[...])).astype(BF16)
    d_gate_pre = (slope * dot(w_out[...], xnorm, 0, 0)).astype(BF16)
    early[0:CH] = dot(normed, d_gate_pre, 1, 1)
    early[CH : 2 * CH] = dot(xnorm, d_out_proj, 1, 1)
    early[2 * CH :] = sums(d_xnorm * xhat, d_xnorm, 2)
    partial[...] = dot(w_gate[...], d_gate_pre, 1, 0)


def back_mine_kernel(parity, own, left, right, da, db):
    place = lax.bitwise_and(parity[0], 1)
    grad = to_matrix(own[...].reshape(16, 8, SUB, CH)).astype(BF16)
    da[...] = dot(grad, right[:, pl.ds(place, 1)].reshape(8 * T, 2 * CH), 1, 0)
    db[...] = from_matrix(dot(grad, left[...], 0, 0)).astype(BF16)


def back_kernel(parity, other, left, right, da_mine, db_mine, send):
    place = lax.bitwise_and(parity[0], 1)
    grad = to_matrix(other[...].reshape(16, 8, SUB, CH)).astype(BF16)
    da = da_mine[...] + dot(grad, right[:, pl.ds(1 - place, 1)].reshape(8 * T, 2 * CH), 1, 0)
    db = from_matrix(dot(grad, left[...], 0, 0)).astype(BF16)
    send[:, :, :, :, :SUB] = from_matrix(da).reshape(2, 2, 4, 8, SUB, CH).astype(BF16)
    send[:, pl.ds(place, 1), :, :, SUB:] = db_mine[...].reshape(2, 1, 4, 8, SUB, CH)
    send[:, pl.ds(1 - place, 1), :, :, SUB:] = db.reshape(2, 1, 4, 8, SUB, CH)


def project_kernel(
    recv, in_proj, coef, normed, zhat, partial, early, send, d_normed, scratch, packed, kept, sem
):
    scratch[...] = recv[...].astype(F32).reshape(2 * CELLS, CH)
    da = from_tiles(scratch, 0, 2 * SUB)
    db = from_tiles(scratch, SUB, 2 * SUB)
    d_proj = jnp.concatenate(
        [
            (grad * coef[part * CH : (part + 1) * CH].astype(F32)).astype(BF16)
            for part, grad in enumerate((da, da, db, db))
        ],
        axis=0,
    )
    g_in = dot(normed[...], d_proj, 1, 1)
    grad = dot(in_proj[...], d_proj, 1, 0) + partial[...]
    kept[...] = grad
    copy = pltpu.make_async_copy(kept, d_normed, sem)
    copy.start()
    for part in range(4):
        packed[pl.ds(part, CH, stride=SUB), :] = g_in[:, part * CH : (part + 1) * CH]
    packed[pl.ds(4, CH, stride=SUB), :] = early[0:CH]
    packed[pl.ds(5, CH, stride=SUB), :] = early[CH : 2 * CH]
    packed[pl.ds(6, CH, stride=SUB), :] = early[2 * CH :] + sums(
        grad * zhat[...].astype(F32), grad, 0
    )
    packed[pl.ds(7, CH, stride=SUB), :] = jnp.zeros((CH, CH), F32)
    send[...] = packed[...].reshape(CH, SUB, CH).astype(BF16)
    copy.wait()


def pair_kernel(d_normed, pair, gain, out):
    scaled, inverse = norm(channel_major(pair))
    grad = norm_back(d_normed[...] * column(gain[...]), scaled, inverse)
    for s in range(SUB):
        block = jnp.transpose(grad[:, s * CH : (s + 1) * CH]).astype(BF16)
        for g in range(GROUPS):
            out[SUB * g + s] = block[g * T : (g + 1) * T]


def total_kernel(recv, after, send):
    total = jnp.sum(recv[...].astype(F32), axis=0, keepdims=True)
    send[...] = jnp.broadcast_to(total, send.shape).astype(BF16)


def unpack_kernel(totals, g_in, g_gate, g_out, ln_in, inner, scratch):
    scratch[...] = totals[...].astype(F32).reshape(CELLS, CH)
    for part in range(4):
        g_in[:, part * CH : (part + 1) * CH] = scratch[pl.ds(part, CH, stride=SUB), :]
    g_gate[...] = scratch[pl.ds(4, CH, stride=SUB), :]
    g_out[...] = scratch[pl.ds(5, CH, stride=SUB), :]
    norms = jnp.transpose(scratch[pl.ds(6, CH, stride=SUB), :])
    ln_in[...] = norms[0:2]
    inner[...] = norms[2:4]


def swap_cores(value):
    return lax.ppermute(value, "depth", [(0, 1), (1, 0)])


def exchange(value, axes=PLANE):
    return lax.all_to_all(value, AXES, 0, 0, tiled=True, axis_index_groups=groups(axes))


def per_device(
    pair,
    grad_out,
    pair_mask,
    ln_in_gain,
    ln_in_bias,
    in_proj,
    w_gate,
    inner_norm_gain,
    inner_norm_bias,
    w_out,
):
    parity = lax.axis_index("depth").astype(jnp.int32).reshape(1)
    in_gain = ln_in_gain.reshape(1, CH)
    in_bias = ln_in_bias.reshape(1, CH)
    x_gain = inner_norm_gain.reshape(1, CH)
    x_bias = inner_norm_bias.reshape(1, CH)
    one = struct((CH, SUB, CH), BF16)
    two = struct((CH, 2 * SUB, CH), BF16)
    square = struct((CH, CH), F32)
    matrix = struct((16 * T, 2 * CH), BF16)
    wide = struct((CH, CELLS), F32)
    narrow = struct((CH, CELLS), BF16)
    tiles = pltpu.VMEM((CELLS, CH), F32)
    pairs_of_tiles = pltpu.VMEM((2 * CELLS, CH), F32)

    (factors,) = call(
        factors_kernel,
        [two],
        pair,
        pair_mask,
        in_gain,
        in_bias,
        in_proj,
        scratch=[pairs_of_tiles],
        fetched=range(5),
    )
    factors, parity = lax.optimization_barrier((factors, parity))
    factors = exchange(factors).reshape(2, 2, 4, 8, 2 * SUB, CH)
    left, x_theirs = call(
        product_theirs_kernel, [matrix, one], parity, factors, spaces={0: pltpu.SMEM}
    )
    x_got = swap_cores(x_theirs)
    right, x_mine = call(
        product_mine_kernel,
        [matrix, struct((CH, SUB, CH), F32)],
        parity,
        factors,
        left,
        spaces={0: pltpu.SMEM},
    )
    right = right.reshape(2, 2, 4 * T, 2 * CH)
    (x_send,) = call(product_kernel, [one], x_mine, x_got)
    x_recv = exchange(x_send)
    (tangent,) = call(
        tangent_kernel,
        [wide],
        pair,
        grad_out,
        in_gain,
        in_bias,
        x_gain,
        w_gate,
        w_out,
        flops=500_000_000,
        fetched=range(7),
    )
    (dx_send,) = call(inner_kernel, [one], x_recv, tangent, scratch=[tiles])
    dx = exchange(dx_send)
    da, db = call(
        back_mine_kernel,
        [struct((16 * T, 2 * CH), F32), struct((8, 8, SUB, CH), BF16)],
        parity,
        dx,
        left,
        right,
        spaces={0: pltpu.SMEM},
    )
    (back_send,) = call(
        back_kernel,
        [struct((2, 2, 4, 8, 2 * SUB, CH), BF16)],
        parity,
        swap_cores(dx),
        left,
        right,
        da,
        db,
        spaces={0: pltpu.SMEM},
    )
    back_send = back_send.reshape(CH, 2 * SUB, CH)
    back = exchange(back_send)
    coef, normed, zhat, partial, early = call(
        output_kernel,
        [struct((4 * CH, CELLS), BF16), narrow, narrow, wide, struct((3 * CH, CH), F32)],
        pair,
        grad_out,
        pair_mask,
        in_gain,
        in_bias,
        x_gain,
        x_bias,
        in_proj,
        w_gate,
        w_out,
        x_recv,
        back_send,
        scratch=[tiles],
        flops=500_000_000,
        fetched=range(10),
        hbm=(11,),
    )
    weights, d_normed = call(
        project_kernel,
        [one, wide],
        back,
        in_proj,
        coef,
        normed,
        zhat,
        partial,
        early,
        scratch=[
            pairs_of_tiles,
            tiles,
            pltpu.VMEM((CH, CELLS), F32),
            pltpu.SemaphoreType.DMA,
        ],
        hbm_outs=(1,),
    )
    weights = exchange(weights.reshape(PARTS, PART, CH), FLAT)
    (grad_pair,) = call(
        pair_kernel,
        [struct((T, T, CH), BF16)],
        d_normed,
        pair,
        in_gain,
        flops=500_000_000,
        fetched=range(3),
    )
    (totals,) = call(
        total_kernel, [struct((PEERS, PART, CH), BF16)], weights, grad_pair, hbm=(1,)
    )
    totals = exchange(totals, UPRIGHT)
    (totals,) = call(
        total_kernel, [struct((PARTS, PART, CH), BF16)], totals, grad_pair, hbm=(1,)
    )
    totals = exchange(totals, FLAT).reshape(CH, SUB, CH)
    g_in, g_gate, g_out, ln_in, inner = call(
        unpack_kernel,
        [struct((CH, 4 * CH), F32), square, square, struct((2, CH), F32), struct((2, CH), F32)],
        totals,
        scratch=[tiles],
    )
    return grad_pair, g_in, g_gate, g_out, ln_in, inner


def solution(mesh):
    fine = Mesh(mesh.devices.reshape(SIZES), AXES)
    cells = P(ROW, COL + ("depth",), None)
    return jax.shard_map(
        per_device,
        mesh=fine,
        in_specs=(cells, cells, P(ROW, COL + ("depth",))) + (P(),) * 7,
        out_specs=(cells,) + (P(),) * 5,
        check_vma=False,
    )
```

```python
import itertools

import jax
import jax.numpy as jnp
from jax import lax
from jax.experimental import pallas as pl
from jax.experimental.pallas import tpu as pltpu
from jax.sharding import Mesh
from jax.sharding import PartitionSpec as P

F32 = jnp.float32
BF16 = jnp.bfloat16
T = 32
CH = 128
CELLS = T * T
SUB = 8
GROUPS = T // SUB
ROW = ("y", "z_lo")
COL = ("x", "z_hi")
SIZES = (4, 4, 4, 2, 2)
AXES = ROW + COL + ("depth",)
PLANE = ("z_lo", "y", "x", "z_hi")
FLAT = ("depth", "y", "x")
UPRIGHT = ("z_lo", "z_hi")
ORIGINS = {PLANE: (2, 2, 2, 1, 0), FLAT: (2, 0, 2, 0, 1), UPRIGHT: (0, 0, 0, 1, 0)}
PARTS = 32
PEERS = 8
PART = CELLS // PARTS


def groups(axes):
    sizes = dict(zip(AXES, SIZES))
    origin = dict(zip(AXES, ORIGINS[axes]))
    rest = [axis for axis in AXES if axis not in axes]
    listed = []
    for outer in itertools.product(*(range(sizes[axis]) for axis in rest)):
        members = []
        for inner in itertools.product(*(range(sizes[axis]) for axis in axes)):
            place = dict(zip(rest, outer))
            for axis, index in zip(axes, inner):
                place[axis] = (index + origin[axis]) % sizes[axis]
            member = 0
            for axis in AXES:
                member = member * sizes[axis] + place[axis]
            members.append(member)
        listed.append(members)
    return listed


def call(kernel, outs, *args, scratch=(), flops=2_000_000, spaces=None, fetched=(), hbm=(), hbm_outs=()):
    spaces = spaces or {}
    fetched = tuple(fetched)
    hbm = fetched + tuple(hbm)
    count = len(args)
    specs = [
        pl.BlockSpec(memory_space=pltpu.HBM if i in hbm else spaces.get(i, pltpu.VMEM))
        for i in range(count)
    ]
    moved = sum(a.size * a.dtype.itemsize for a in args)
    moved += sum(o.size * o.dtype.itemsize for o in outs)
    args = [
        pltpu.with_memory_space_constraint(a, pltpu.HBM) if i in hbm else a
        for i, a in enumerate(args)
    ]

    def body(*refs):
        if not fetched:
            return kernel(*refs)
        local = refs[len(refs) - 1 - len(fetched) : -1]
        refs, sems = refs[: len(refs) - 1 - len(fetched)], refs[-1]
        inputs = list(refs[:count])
        copies = [
            pltpu.make_async_copy(inputs[i], target, sems.at[place])
            for place, (i, target) in enumerate(zip(fetched, local))
        ]
        for copy in copies:
            copy.start()
        for copy in copies:
            copy.wait()
        for i, target in zip(fetched, local):
            inputs[i] = target
        return kernel(*inputs, *refs[count:])

    extra = [pltpu.VMEM(args[i].shape, args[i].dtype) for i in fetched]
    if fetched:
        extra.append(pltpu.SemaphoreType.DMA((len(fetched),)))
    return pl.pallas_call(
        body,
        out_shape=[pltpu.HBM(o.shape, o.dtype) if i in hbm_outs else o for i, o in enumerate(outs)],
        in_specs=specs,
        out_specs=[
            pl.BlockSpec(memory_space=pltpu.HBM if i in hbm_outs else pltpu.VMEM)
            for i in range(len(outs))
        ],
        scratch_shapes=list(scratch) + extra,
        compiler_params=pltpu.CompilerParams(vmem_limit_bytes=32 * 1024 * 1024),
        cost_estimate=pl.CostEstimate(flops=flops, bytes_accessed=moved, transcendentals=0),
    )(*args)


def struct(shape, dtype):
    return jax.ShapeDtypeStruct(shape, dtype)


def column(row):
    return jnp.transpose(jnp.broadcast_to(row, (CH, CH)))[:, :1]


def dot(a, b, ca, cb):
    return lax.dot_general(a, b, (((ca,), (cb,)), ((), ())), preferred_element_type=F32)


def channel_major(ref):
    chunks = []
    for s in range(SUB):
        block = jnp.concatenate([ref[SUB * g + s] for g in range(GROUPS)], axis=0)
        chunks.append(jnp.transpose(block.astype(F32)))
    return jnp.concatenate(chunks, axis=1)


def to_tiles(value, scratch, first, stride):
    for s in range(SUB):
        scratch[pl.ds(first + s, CH, stride=stride), :] = value[:, s * CH : (s + 1) * CH]


def from_tiles(scratch, first, stride):
    return jnp.concatenate(
        [scratch[pl.ds(first + s, CH, stride=stride), :] for s in range(SUB)], axis=1
    )


def norm(value):
    centre = value - jnp.mean(value, axis=0, keepdims=True)
    inverse = lax.rsqrt(jnp.mean(centre * centre, axis=0, keepdims=True) + 1e-05)
    return centre * inverse, inverse


def norm_back(tangent, scaled, inverse):
    first = jnp.mean(tangent, axis=0, keepdims=True)
    second = jnp.mean(tangent * scaled, axis=0, keepdims=True)
    return inverse * (tangent - first - scaled * second)


def swap_groups(parts):
    a, b, c, d = parts
    axis = a.ndim - 1
    lane = lax.broadcasted_iota(jnp.int32, a.shape, axis)
    low = lane < 64
    even = (lane & 32) == 0
    a, c = jnp.where(low, a, pltpu.roll(c, 64, axis)), jnp.where(low, pltpu.roll(a, 64, axis), c)
    b, d = jnp.where(low, b, pltpu.roll(d, 64, axis)), jnp.where(low, pltpu.roll(b, 64, axis), d)
    a, b = jnp.where(even, a, pltpu.roll(b, 32, axis)), jnp.where(even, pltpu.roll(a, 96, axis), b)
    c, d = jnp.where(even, c, pltpu.roll(d, 32, axis)), jnp.where(even, pltpu.roll(c, 96, axis), d)
    return a, b, c, d


def to_matrix(tiles):
    blocks = tiles.shape[0]
    halves = []
    for half in range(2):
        parts = [tiles[:, 2 * part + half].astype(F32) for part in range(4)]
        rows = jnp.stack(swap_groups(parts), axis=1)
        halves.append(rows.reshape(blocks * T, CH))
    return jnp.concatenate(halves, axis=1)


def from_matrix(matrix):
    blocks = matrix.shape[0] // T
    halves = []
    for half in range(2):
        rows = matrix[:, half * CH : (half + 1) * CH].reshape(blocks, GROUPS, SUB, CH)
        halves.append(swap_groups([rows[:, g] for g in range(GROUPS)]))
    return jnp.stack([halves[half][part] for part in range(4) for half in range(2)], axis=1)


def normalise(pair, gain, bias):
    scaled, inverse = norm(channel_major(pair))
    return scaled, inverse, (scaled * column(gain[...]) + column(bias[...])).astype(BF16)


def factors_of(normed, mask, in_proj):
    proj = dot(in_proj[...], normed, 0, 0)
    flags = mask[...].astype(F32)
    tile = jnp.concatenate([flags[SUB * g : SUB * (g + 1)] for g in range(GROUPS)], axis=1)
    m = jnp.concatenate([tile[s : s + 1] for s in range(SUB)], axis=1)
    sides = []
    for side in range(2):
        val = proj[2 * side * CH : (2 * side + 1) * CH]
        sig = jax.nn.sigmoid(proj[(2 * side + 1) * CH : (2 * side + 2) * CH])
        gated = sig * m
        sides.append((gated, gated * val, 1.0 - sig))
    return sides


def factors_kernel(pair, mask, gain, bias, in_proj, send, scratch):
    normed = normalise(pair, gain, bias)[2]
    for side, (_, factor, _) in enumerate(factors_of(normed, mask, in_proj)):
        to_tiles(factor, scratch, side * SUB, 2 * SUB)
    send[...] = scratch[...].reshape(CH, 2 * SUB, CH).astype(BF16)


def gated_grad(grad_out, normed, w_gate):
    gate = jax.nn.sigmoid(dot(w_gate[...], normed, 0, 0))
    moved = channel_major(grad_out) * gate
    return moved.astype(BF16), moved * (1.0 - gate)


def tangent_kernel(pair, grad_out, gain, bias, x_gain, w_gate, w_out, tangent):
    normed = normalise(pair, gain, bias)[2]
    d_out_proj, _ = gated_grad(grad_out, normed, w_gate)
    tangent[...] = dot(w_out[...], d_out_proj, 1, 0) * column(x_gain[...])


def product_theirs_kernel(parity, own, left_out, theirs):
    other = 1 - lax.bitwise_and(parity[0], 1)
    left = to_matrix(own[:, :, :, :, :SUB].reshape(16, 8, SUB, CH)).astype(BF16)
    left_out[...] = left
    right = to_matrix(own[:, pl.ds(other, 1), :, :, SUB:].reshape(8, 8, SUB, CH)).astype(BF16)
    theirs[...] = from_matrix(dot(left, right, 1, 1)).reshape(CH, SUB, CH).astype(BF16)


def product_mine_kernel(parity, own, left, right_out, mine):
    place = lax.bitwise_and(parity[0], 1)
    right_out[...] = to_matrix(own[:, :, :, :, SUB:].reshape(16, 8, SUB, CH)).astype(BF16)
    right = to_matrix(own[:, pl.ds(place, 1), :, :, SUB:].reshape(8, 8, SUB, CH)).astype(BF16)
    mine[...] = from_matrix(dot(left[...], right, 1, 1)).reshape(CH, SUB, CH)


def product_kernel(mine, got, send):
    send[...] = (mine[...] + got[...].astype(F32)).astype(BF16)


def inner_kernel(recv, tangent, send, scratch):
    scratch[...] = recv[...].astype(F32).reshape(CELLS, CH)
    scaled, inverse = norm(from_tiles(scratch, 0, SUB))
    to_tiles(norm_back(tangent[...], scaled, inverse), scratch, 0, SUB)
    send[...] = scratch[...].reshape(CH, SUB, CH).astype(BF16)


def sums(first, second, place):
    lane = lax.broadcasted_iota(jnp.int32, (CH, CH), 1)
    a = jnp.sum(first, axis=1, keepdims=True)
    b = jnp.sum(second, axis=1, keepdims=True)
    return jnp.where(lane == place, a, jnp.where(lane == place + 1, b, 0.0))


def output_kernel(
    pair,
    grad_out,
    mask,
    gain,
    bias,
    x_gain,
    x_bias,
    in_proj,
    w_gate,
    w_out,
    x_recv,
    after,
    coef,
    normed_out,
    zhat,
    partial,
    early,
    scratch,
):
    scaled, _, normed = normalise(pair, gain, bias)
    zhat[...] = scaled.astype(BF16)
    normed_out[...] = normed
    for side, (gated, factor, rest) in enumerate(factors_of(normed, mask, in_proj)):
        coef[2 * side * CH : (2 * side + 1) * CH] = gated.astype(BF16)
        coef[(2 * side + 1) * CH : (2 * side + 2) * CH] = (factor * rest).astype(BF16)
    d_out_proj, slope = gated_grad(grad_out, normed, w_gate)
    d_xnorm = dot(w_out[...], d_out_proj, 1, 0)
    scratch[...] = x_recv[...].astype(F32).reshape(CELLS, CH)
    xhat, _ = norm(from_tiles(scratch, 0, SUB))
    xnorm = (xhat * column(x_gain[...]) + column(x_bias[...])).astype(BF16)
    d_gate_pre = (slope * dot(w_out[...], xnorm, 0, 0)).astype(BF16)
    early[0:CH] = dot(normed, d_gate_pre, 1, 1)
    early[CH : 2 * CH] = dot(xnorm, d_out_proj, 1, 1)
    early[2 * CH :] = sums(d_xnorm * xhat, d_xnorm, 2)
    partial[...] = dot(w_gate[...], d_gate_pre, 1, 0)


def back_mine_kernel(parity, own, left, right, da, db):
    place = lax.bitwise_and(parity[0], 1)
    grad = to_matrix(own[...].reshape(16, 8, SUB, CH)).astype(BF16)
    da[...] = dot(grad, right[:, pl.ds(place, 1)].reshape(8 * T, 2 * CH), 1, 0)
    db[...] = from_matrix(dot(grad, left[...], 0, 0)).astype(BF16)


def back_kernel(parity, other, left, right, da_mine, db_mine, send):
    place = lax.bitwise_and(parity[0], 1)
    grad = to_matrix(other[...].reshape(16, 8, SUB, CH)).astype(BF16)
    da = da_mine[...] + dot(grad, right[:, pl.ds(1 - place, 1)].reshape(8 * T, 2 * CH), 1, 0)
    db = from_matrix(dot(grad, left[...], 0, 0)).astype(BF16)
    send[:, :, :, :, :SUB] = from_matrix(da).reshape(2, 2, 4, 8, SUB, CH).astype(BF16)
    send[:, pl.ds(place, 1), :, :, SUB:] = db_mine[...].reshape(2, 1, 4, 8, SUB, CH)
    send[:, pl.ds(1 - place, 1), :, :, SUB:] = db.reshape(2, 1, 4, 8, SUB, CH)


def project_kernel(
    recv, in_proj, coef, normed, zhat, partial, early, send, d_normed, scratch, packed, kept, sem
):
    scratch[...] = recv[...].astype(F32).reshape(2 * CELLS, CH)
    da = from_tiles(scratch, 0, 2 * SUB)
    db = from_tiles(scratch, SUB, 2 * SUB)
    d_proj = jnp.concatenate(
        [
            (grad * coef[part * CH : (part + 1) * CH].astype(F32)).astype(BF16)
            for part, grad in enumerate((da, da, db, db))
        ],
        axis=0,
    )
    g_in = dot(normed[...], d_proj, 1, 1)
    grad = dot(in_proj[...], d_proj, 1, 0) + partial[...]
    kept[...] = grad
    copy = pltpu.make_async_copy(kept, d_normed, sem)
    copy.start()
    for part in range(4):
        packed[pl.ds(part, CH, stride=SUB), :] = g_in[:, part * CH : (part + 1) * CH]
    packed[pl.ds(4, CH, stride=SUB), :] = early[0:CH]
    packed[pl.ds(5, CH, stride=SUB), :] = early[CH : 2 * CH]
    packed[pl.ds(6, CH, stride=SUB), :] = early[2 * CH :] + sums(
        grad * zhat[...].astype(F32), grad, 0
    )
    packed[pl.ds(7, CH, stride=SUB), :] = jnp.zeros((CH, CH), F32)
    send[...] = packed[...].reshape(CH, SUB, CH).astype(BF16)
    copy.wait()


def pair_kernel(d_normed, pair, gain, out):
    scaled, inverse = norm(channel_major(pair))
    grad = norm_back(d_normed[...] * column(gain[...]), scaled, inverse)
    for s in range(SUB):
        block = jnp.transpose(grad[:, s * CH : (s + 1) * CH]).astype(BF16)
        for g in range(GROUPS):
            out[SUB * g + s] = block[g * T : (g + 1) * T]


def total_kernel(recv, after, send):
    total = jnp.sum(recv[...].astype(F32), axis=0, keepdims=True)
    send[...] = jnp.broadcast_to(total, send.shape).astype(BF16)


def unpack_kernel(totals, g_in, g_gate, g_out, ln_in, inner, scratch):
    scratch[...] = totals[...].astype(F32).reshape(CELLS, CH)
    for part in range(4):
        g_in[:, part * CH : (part + 1) * CH] = scratch[pl.ds(part, CH, stride=SUB), :]
    g_gate[...] = scratch[pl.ds(4, CH, stride=SUB), :]
    g_out[...] = scratch[pl.ds(5, CH, stride=SUB), :]
    norms = jnp.transpose(scratch[pl.ds(6, CH, stride=SUB), :])
    ln_in[...] = norms[0:2]
    inner[...] = norms[2:4]


def swap_cores(value):
    return lax.ppermute(value, "depth", [(0, 1), (1, 0)])


def exchange(value, axes=PLANE):
    return lax.all_to_all(value, AXES, 0, 0, tiled=True, axis_index_groups=groups(axes))


def per_device(
    pair,
    grad_out,
    pair_mask,
    ln_in_gain,
    ln_in_bias,
    in_proj,
    w_gate,
    inner_norm_gain,
    inner_norm_bias,
    w_out,
):
    parity = lax.axis_index("depth").astype(jnp.int32).reshape(1)
    in_gain = ln_in_gain.reshape(1, CH)
    in_bias = ln_in_bias.reshape(1, CH)
    x_gain = inner_norm_gain.reshape(1, CH)
    x_bias = inner_norm_bias.reshape(1, CH)
    one = struct((CH, SUB, CH), BF16)
    two = struct((CH, 2 * SUB, CH), BF16)
    square = struct((CH, CH), F32)
    matrix = struct((16 * T, 2 * CH), BF16)
    wide = struct((CH, CELLS), F32)
    narrow = struct((CH, CELLS), BF16)
    tiles = pltpu.VMEM((CELLS, CH), F32)
    pairs_of_tiles = pltpu.VMEM((2 * CELLS, CH), F32)

    (factors,) = call(
        factors_kernel,
        [two],
        pair,
        pair_mask,
        in_gain,
        in_bias,
        in_proj,
        scratch=[pairs_of_tiles],
        fetched=range(5),
    )
    factors, parity = lax.optimization_barrier((factors, parity))
    factors = exchange(factors).reshape(2, 2, 4, 8, 2 * SUB, CH)
    left, x_theirs = call(
        product_theirs_kernel, [matrix, one], parity, factors, spaces={0: pltpu.SMEM}
    )
    x_got = swap_cores(x_theirs)
    right, x_mine = call(
        product_mine_kernel,
        [matrix, struct((CH, SUB, CH), F32)],
        parity,
        factors,
        left,
        spaces={0: pltpu.SMEM},
    )
    right = right.reshape(2, 2, 4 * T, 2 * CH)
    (x_send,) = call(product_kernel, [one], x_mine, x_got)
    x_recv = exchange(x_send)
    (tangent,) = call(
        tangent_kernel,
        [wide],
        pair,
        grad_out,
        in_gain,
        in_bias,
        x_gain,
        w_gate,
        w_out,
        flops=500_000_000,
        fetched=range(7),
    )
    (dx_send,) = call(inner_kernel, [one], x_recv, tangent, scratch=[tiles])
    dx = exchange(dx_send)
    da, db = call(
        back_mine_kernel,
        [struct((16 * T, 2 * CH), F32), struct((8, 8, SUB, CH), BF16)],
        parity,
        dx,
        left,
        right,
        spaces={0: pltpu.SMEM},
    )
    (back_send,) = call(
        back_kernel,
        [struct((2, 2, 4, 8, 2 * SUB, CH), BF16)],
        parity,
        swap_cores(dx),
        left,
        right,
        da,
        db,
        spaces={0: pltpu.SMEM},
    )
    back_send = back_send.reshape(CH, 2 * SUB, CH)
    back = exchange(back_send)
    coef, normed, zhat, partial, early = call(
        output_kernel,
        [struct((4 * CH, CELLS), BF16), narrow, narrow, wide, struct((3 * CH, CH), F32)],
        pair,
        grad_out,
        pair_mask,
        in_gain,
        in_bias,
        x_gain,
        x_bias,
        in_proj,
        w_gate,
        w_out,
        x_recv,
        back_send,
        scratch=[tiles],
        flops=500_000_000,
        fetched=range(10),
        hbm=(11,),
    )
    weights, d_normed = call(
        project_kernel,
        [one, wide],
        back,
        in_proj,
        coef,
        normed,
        zhat,
        partial,
        early,
        scratch=[
            pairs_of_tiles,
            tiles,
            pltpu.VMEM((CH, CELLS), F32),
            pltpu.SemaphoreType.DMA,
        ],
        hbm_outs=(1,),
    )
    weights = exchange(weights.reshape(PARTS, PART, CH), FLAT)
    (grad_pair,) = call(
        pair_kernel,
        [struct((T, T, CH), BF16)],
        d_normed,
        pair,
        in_gain,
        flops=500_000_000,
        fetched=range(3),
    )
    (totals,) = call(
        total_kernel, [struct((PEERS, PART, CH), BF16)], weights, grad_pair, hbm=(1,)
    )
    totals = exchange(totals, UPRIGHT)
    (totals,) = call(
        total_kernel, [struct((PARTS, PART, CH), BF16)], totals, grad_pair, hbm=(1,)
    )
    totals = exchange(totals, FLAT).reshape(CH, SUB, CH)
    g_in, g_gate, g_out, ln_in, inner = call(
        unpack_kernel,
        [struct((CH, 4 * CH), F32), square, square, struct((2, CH), F32), struct((2, CH), F32)],
        totals,
        scratch=[tiles],
    )
    return grad_pair, g_in, g_gate, g_out, ln_in, inner


def solution(mesh):
    fine = Mesh(mesh.devices.reshape(SIZES), AXES)
    cells = P(ROW, COL + ("depth",), None)
    return jax.shard_map(
        per_device,
        mesh=fine,
        in_specs=(cells, cells, P(ROW, COL + ("depth",))) + (P(),) * 7,
        out_specs=(cells,) + (P(),) * 5,
        check_vma=False,
    )
```

```python
import itertools

import jax
import jax.numpy as jnp
from jax import lax
from jax.experimental import pallas as pl
from jax.experimental.pallas import tpu as pltpu
from jax.sharding import Mesh
from jax.sharding import PartitionSpec as P

F32 = jnp.float32
BF16 = jnp.bfloat16
T = 32
CH = 128
CELLS = T * T
SUB = 8
GROUPS = T // SUB
ROW = ("y", "z_lo")
COL = ("x", "z_hi")
SIZES = (4, 4, 4, 2, 2)
AXES = ROW + COL + ("depth",)
PLANE = ("z_lo", "y", "x", "z_hi")
FLAT = ("depth", "y", "x")
UPRIGHT = ("z_lo", "z_hi")
ORIGINS = {PLANE: (2, 2, 2, 1, 0), FLAT: (2, 0, 2, 0, 1), UPRIGHT: (0, 0, 0, 1, 0)}
PARTS = 32
PEERS = 8
PART = CELLS // PARTS


def groups(axes):
    sizes = dict(zip(AXES, SIZES))
    origin = dict(zip(AXES, ORIGINS[axes]))
    rest = [axis for axis in AXES if axis not in axes]
    listed = []
    for outer in itertools.product(*(range(sizes[axis]) for axis in rest)):
        members = []
        for inner in itertools.product(*(range(sizes[axis]) for axis in axes)):
            place = dict(zip(rest, outer))
            for axis, index in zip(axes, inner):
                place[axis] = (index + origin[axis]) % sizes[axis]
            member = 0
            for axis in AXES:
                member = member * sizes[axis] + place[axis]
            members.append(member)
        listed.append(members)
    return listed


def call(kernel, outs, *args, scratch=(), flops=2_000_000, spaces=None, fetched=(), hbm=(), hbm_outs=()):
    spaces = spaces or {}
    fetched = tuple(fetched)
    hbm = fetched + tuple(hbm)
    count = len(args)
    specs = [
        pl.BlockSpec(memory_space=pltpu.HBM if i in hbm else spaces.get(i, pltpu.VMEM))
        for i in range(count)
    ]
    moved = sum(a.size * a.dtype.itemsize for a in args)
    moved += sum(o.size * o.dtype.itemsize for o in outs)
    args = [
        pltpu.with_memory_space_constraint(a, pltpu.HBM) if i in hbm else a
        for i, a in enumerate(args)
    ]

    def body(*refs):
        if not fetched:
            return kernel(*refs)
        local = refs[len(refs) - 1 - len(fetched) : -1]
        refs, sems = refs[: len(refs) - 1 - len(fetched)], refs[-1]
        inputs = list(refs[:count])
        copies = [
            pltpu.make_async_copy(inputs[i], target, sems.at[place])
            for place, (i, target) in enumerate(zip(fetched, local))
        ]
        for copy in copies:
            copy.start()
        for copy in copies:
            copy.wait()
        for i, target in zip(fetched, local):
            inputs[i] = target
        return kernel(*inputs, *refs[count:])

    extra = [pltpu.VMEM(args[i].shape, args[i].dtype) for i in fetched]
    if fetched:
        extra.append(pltpu.SemaphoreType.DMA((len(fetched),)))
    return pl.pallas_call(
        body,
        out_shape=[pltpu.HBM(o.shape, o.dtype) if i in hbm_outs else o for i, o in enumerate(outs)],
        in_specs=specs,
        out_specs=[
            pl.BlockSpec(memory_space=pltpu.HBM if i in hbm_outs else pltpu.VMEM)
            for i in range(len(outs))
        ],
        scratch_shapes=list(scratch) + extra,
        compiler_params=pltpu.CompilerParams(vmem_limit_bytes=32 * 1024 * 1024),
        cost_estimate=pl.CostEstimate(flops=flops, bytes_accessed=moved, transcendentals=0),
    )(*args)


def struct(shape, dtype):
    return jax.ShapeDtypeStruct(shape, dtype)


def column(row):
    return jnp.transpose(jnp.broadcast_to(row, (CH, CH)))[:, :1]


def dot(a, b, ca, cb):
    return lax.dot_general(a, b, (((ca,), (cb,)), ((), ())), preferred_element_type=F32)


def channel_major(ref):
    chunks = []
    for s in range(SUB):
        block = jnp.concatenate([ref[SUB * g + s] for g in range(GROUPS)], axis=0)
        chunks.append(jnp.transpose(block.astype(F32)))
    return jnp.concatenate(chunks, axis=1)


def to_tiles(value, scratch, first, stride):
    for s in range(SUB):
        scratch[pl.ds(first + s, CH, stride=stride), :] = value[:, s * CH : (s + 1) * CH]


def from_tiles(scratch, first, stride):
    return jnp.concatenate(
        [scratch[pl.ds(first + s, CH, stride=stride), :] for s in range(SUB)], axis=1
    )


def norm(value):
    centre = value - jnp.mean(value, axis=0, keepdims=True)
    inverse = lax.rsqrt(jnp.mean(centre * centre, axis=0, keepdims=True) + 1e-05)
    return centre * inverse, inverse


def norm_back(tangent, scaled, inverse):
    first = jnp.mean(tangent, axis=0, keepdims=True)
    second = jnp.mean(tangent * scaled, axis=0, keepdims=True)
    return inverse * (tangent - first - scaled * second)


def swap_groups(parts):
    a, b, c, d = parts
    axis = a.ndim - 1
    lane = lax.broadcasted_iota(jnp.int32, a.shape, axis)
    low = lane < 64
    even = (lane & 32) == 0
    a, c = jnp.where(low, a, pltpu.roll(c, 64, axis)), jnp.where(low, pltpu.roll(a, 64, axis), c)
    b, d = jnp.where(low, b, pltpu.roll(d, 64, axis)), jnp.where(low, pltpu.roll(b, 64, axis), d)
    a, b = jnp.where(even, a, pltpu.roll(b, 32, axis)), jnp.where(even, pltpu.roll(a, 96, axis), b)
    c, d = jnp.where(even, c, pltpu.roll(d, 32, axis)), jnp.where(even, pltpu.roll(c, 96, axis), d)
    return a, b, c, d


def to_matrix(tiles):
    blocks = tiles.shape[0]
    halves = []
    for half in range(2):
        parts = [tiles[:, 2 * part + half].astype(F32) for part in range(4)]
        rows = jnp.stack(swap_groups(parts), axis=1)
        halves.append(rows.reshape(blocks * T, CH))
    return jnp.concatenate(halves, axis=1)


def from_matrix(matrix):
    blocks = matrix.shape[0] // T
    halves = []
    for half in range(2):
        rows = matrix[:, half * CH : (half + 1) * CH].reshape(blocks, GROUPS, SUB, CH)
        halves.append(swap_groups([rows[:, g] for g in range(GROUPS)]))
    return jnp.stack([halves[half][part] for part in range(4) for half in range(2)], axis=1)


def normalise(pair, gain, bias):
    scaled, inverse = norm(channel_major(pair))
    return scaled, inverse, (scaled * column(gain[...]) + column(bias[...])).astype(BF16)


def factors_of(normed, mask, in_proj):
    proj = dot(in_proj[...], normed, 0, 0)
    flags = mask[...].astype(F32)
    tile = jnp.concatenate([flags[SUB * g : SUB * (g + 1)] for g in range(GROUPS)], axis=1)
    m = jnp.concatenate([tile[s : s + 1] for s in range(SUB)], axis=1)
    sides = []
    for side in range(2):
        val = proj[2 * side * CH : (2 * side + 1) * CH]
        sig = jax.nn.sigmoid(proj[(2 * side + 1) * CH : (2 * side + 2) * CH])
        gated = sig * m
        sides.append((gated, gated * val, 1.0 - sig))
    return sides


def factors_kernel(
    pair, grad_out, mask, gain, bias, x_gain, in_proj, w_gate, w_out, send, tangent, scratch
):
    normed = normalise(pair, gain, bias)[2]
    for side, (_, factor, _) in enumerate(factors_of(normed, mask, in_proj)):
        to_tiles(factor, scratch, side * SUB, 2 * SUB)
    send[...] = scratch[...].reshape(CH, 2 * SUB, CH).astype(BF16)
    d_out_proj, _ = gated_grad(grad_out, normed, w_gate)
    tangent[...] = dot(w_out[...], d_out_proj, 1, 0) * column(x_gain[...])


def gated_grad(grad_out, normed, w_gate):
    gate = jax.nn.sigmoid(dot(w_gate[...], normed, 0, 0))
    moved = channel_major(grad_out) * gate
    return moved.astype(BF16), moved * (1.0 - gate)


def product_theirs_kernel(parity, own, left_out, theirs):
    other = 1 - lax.bitwise_and(parity[0], 1)
    left = to_matrix(own[:, :, :, :, :SUB].reshape(16, 8, SUB, CH)).astype(BF16)
    left_out[...] = left
    right = to_matrix(own[:, pl.ds(other, 1), :, :, SUB:].reshape(8, 8, SUB, CH)).astype(BF16)
    theirs[...] = from_matrix(dot(left, right, 1, 1)).reshape(CH, SUB, CH).astype(BF16)


def product_mine_kernel(parity, own, left, right_out, mine):
    place = lax.bitwise_and(parity[0], 1)
    right_out[...] = to_matrix(own[:, :, :, :, SUB:].reshape(16, 8, SUB, CH)).astype(BF16)
    right = to_matrix(own[:, pl.ds(place, 1), :, :, SUB:].reshape(8, 8, SUB, CH)).astype(BF16)
    mine[...] = from_matrix(dot(left[...], right, 1, 1)).reshape(CH, SUB, CH)


def product_kernel(mine, got, send):
    send[...] = (mine[...] + got[...].astype(F32)).astype(BF16)


def inner_kernel(recv, tangent, send, scratch):
    scratch[...] = recv[...].astype(F32).reshape(CELLS, CH)
    scaled, inverse = norm(from_tiles(scratch, 0, SUB))
    to_tiles(norm_back(tangent[...], scaled, inverse), scratch, 0, SUB)
    send[...] = scratch[...].reshape(CH, SUB, CH).astype(BF16)


def sums(first, second, place):
    lane = lax.broadcasted_iota(jnp.int32, (CH, CH), 1)
    a = jnp.sum(first, axis=1, keepdims=True)
    b = jnp.sum(second, axis=1, keepdims=True)
    return jnp.where(lane == place, a, jnp.where(lane == place + 1, b, 0.0))


def output_kernel(
    pair,
    grad_out,
    mask,
    gain,
    bias,
    x_gain,
    x_bias,
    in_proj,
    w_gate,
    w_out,
    x_recv,
    after,
    coef,
    normed_out,
    zhat,
    partial,
    early,
    scratch,
):
    scaled, _, normed = normalise(pair, gain, bias)
    zhat[...] = scaled.astype(BF16)
    normed_out[...] = normed
    for side, (gated, factor, rest) in enumerate(factors_of(normed, mask, in_proj)):
        coef[2 * side * CH : (2 * side + 1) * CH] = gated.astype(BF16)
        coef[(2 * side + 1) * CH : (2 * side + 2) * CH] = (factor * rest).astype(BF16)
    d_out_proj, slope = gated_grad(grad_out, normed, w_gate)
    d_xnorm = dot(w_out[...], d_out_proj, 1, 0)
    scratch[...] = x_recv[...].astype(F32).reshape(CELLS, CH)
    xhat, _ = norm(from_tiles(scratch, 0, SUB))
    xnorm = (xhat * column(x_gain[...]) + column(x_bias[...])).astype(BF16)
    d_gate_pre = (slope * dot(w_out[...], xnorm, 0, 0)).astype(BF16)
    early[0:CH] = dot(normed, d_gate_pre, 1, 1)
    early[CH : 2 * CH] = dot(xnorm, d_out_proj, 1, 1)
    early[2 * CH :] = sums(d_xnorm * xhat, d_xnorm, 2)
    partial[...] = dot(w_gate[...], d_gate_pre, 1, 0)


def back_mine_kernel(parity, own, left, right, da, db):
    place = lax.bitwise_and(parity[0], 1)
    grad = to_matrix(own[...].reshape(16, 8, SUB, CH)).astype(BF16)
    da[...] = dot(grad, right[:, pl.ds(place, 1)].reshape(8 * T, 2 * CH), 1, 0)
    db[...] = from_matrix(dot(grad, left[...], 0, 0)).astype(BF16)


def back_kernel(parity, other, left, right, da_mine, db_mine, send):
    place = lax.bitwise_and(parity[0], 1)
    grad = to_matrix(other[...].reshape(16, 8, SUB, CH)).astype(BF16)
    da = da_mine[...] + dot(grad, right[:, pl.ds(1 - place, 1)].reshape(8 * T, 2 * CH), 1, 0)
    db = from_matrix(dot(grad, left[...], 0, 0)).astype(BF16)
    send[:, :, :, :, :SUB] = from_matrix(da).reshape(2, 2, 4, 8, SUB, CH).astype(BF16)
    send[:, pl.ds(place, 1), :, :, SUB:] = db_mine[...].reshape(2, 1, 4, 8, SUB, CH)
    send[:, pl.ds(1 - place, 1), :, :, SUB:] = db.reshape(2, 1, 4, 8, SUB, CH)


def project_kernel(
    recv, in_proj, coef, normed, zhat, partial, early, send, d_normed, scratch, packed, kept, sem
):
    scratch[...] = recv[...].astype(F32).reshape(2 * CELLS, CH)
    da = from_tiles(scratch, 0, 2 * SUB)
    db = from_tiles(scratch, SUB, 2 * SUB)
    d_proj = jnp.concatenate(
        [
            (grad * coef[part * CH : (part + 1) * CH].astype(F32)).astype(BF16)
            for part, grad in enumerate((da, da, db, db))
        ],
        axis=0,
    )
    g_in = dot(normed[...], d_proj, 1, 1)
    grad = dot(in_proj[...], d_proj, 1, 0) + partial[...]
    kept[...] = grad
    copy = pltpu.make_async_copy(kept, d_normed, sem)
    copy.start()
    for part in range(4):
        packed[pl.ds(part, CH, stride=SUB), :] = g_in[:, part * CH : (part + 1) * CH]
    packed[pl.ds(4, CH, stride=SUB), :] = early[0:CH]
    packed[pl.ds(5, CH, stride=SUB), :] = early[CH : 2 * CH]
    packed[pl.ds(6, CH, stride=SUB), :] = early[2 * CH :] + sums(
        grad * zhat[...].astype(F32), grad, 0
    )
    packed[pl.ds(7, CH, stride=SUB), :] = jnp.zeros((CH, CH), F32)
    send[...] = packed[...].reshape(CH, SUB, CH).astype(BF16)
    copy.wait()


def pair_kernel(d_normed, pair, gain, out):
    scaled, inverse = norm(channel_major(pair))
    grad = norm_back(d_normed[...] * column(gain[...]), scaled, inverse)
    for s in range(SUB):
        block = jnp.transpose(grad[:, s * CH : (s + 1) * CH]).astype(BF16)
        for g in range(GROUPS):
            out[SUB * g + s] = block[g * T : (g + 1) * T]


def total_kernel(recv, *refs):
    send = refs[-1]
    total = jnp.sum(recv[...].astype(F32), axis=0, keepdims=True)
    send[...] = jnp.broadcast_to(total, send.shape).astype(BF16)


def unpack_kernel(totals, g_in, g_gate, g_out, ln_in, inner, scratch):
    scratch[...] = totals[...].astype(F32).reshape(CELLS, CH)
    for part in range(4):
        g_in[:, part * CH : (part + 1) * CH] = scratch[pl.ds(part, CH, stride=SUB), :]
    g_gate[...] = scratch[pl.ds(4, CH, stride=SUB), :]
    g_out[...] = scratch[pl.ds(5, CH, stride=SUB), :]
    norms = jnp.transpose(scratch[pl.ds(6, CH, stride=SUB), :])
    ln_in[...] = norms[0:2]
    inner[...] = norms[2:4]


def swap_cores(value):
    return lax.ppermute(value, "depth", [(0, 1), (1, 0)])


def exchange(value, axes=PLANE):
    return lax.all_to_all(value, AXES, 0, 0, tiled=True, axis_index_groups=groups(axes))


def per_device(
    pair,
    grad_out,
    pair_mask,
    ln_in_gain,
    ln_in_bias,
    in_proj,
    w_gate,
    inner_norm_gain,
    inner_norm_bias,
    w_out,
):
    parity = lax.axis_index("depth").astype(jnp.int32).reshape(1)
    in_gain = ln_in_gain.reshape(1, CH)
    in_bias = ln_in_bias.reshape(1, CH)
    x_gain = inner_norm_gain.reshape(1, CH)
    x_bias = inner_norm_bias.reshape(1, CH)
    one = struct((CH, SUB, CH), BF16)
    two = struct((CH, 2 * SUB, CH), BF16)
    square = struct((CH, CH), F32)
    matrix = struct((16 * T, 2 * CH), BF16)
    wide = struct((CH, CELLS), F32)
    narrow = struct((CH, CELLS), BF16)
    tiles = pltpu.VMEM((CELLS, CH), F32)
    pairs_of_tiles = pltpu.VMEM((2 * CELLS, CH), F32)

    factors, tangent = call(
        factors_kernel,
        [two, wide],
        pair,
        grad_out,
        pair_mask,
        in_gain,
        in_bias,
        x_gain,
        in_proj,
        w_gate,
        w_out,
        scratch=[pairs_of_tiles],
        fetched=range(9),
    )
    factors, parity = lax.optimization_barrier((factors, parity))
    factors = exchange(factors).reshape(2, 2, 4, 8, 2 * SUB, CH)
    left, x_theirs = call(
        product_theirs_kernel, [matrix, one], parity, factors, spaces={0: pltpu.SMEM}
    )
    x_got = swap_cores(x_theirs)
    right, x_mine = call(
        product_mine_kernel,
        [matrix, struct((CH, SUB, CH), F32)],
        parity,
        factors,
        left,
        spaces={0: pltpu.SMEM},
    )
    right = right.reshape(2, 2, 4 * T, 2 * CH)
    (x_send,) = call(product_kernel, [one], x_mine, x_got)
    x_recv = exchange(x_send)
    (dx_send,) = call(inner_kernel, [one], x_recv, tangent, scratch=[tiles])
    dx = exchange(dx_send)
    da, db = call(
        back_mine_kernel,
        [struct((16 * T, 2 * CH), F32), struct((8, 8, SUB, CH), BF16)],
        parity,
        dx,
        left,
        right,
        spaces={0: pltpu.SMEM},
    )
    (back_send,) = call(
        back_kernel,
        [struct((2, 2, 4, 8, 2 * SUB, CH), BF16)],
        parity,
        swap_cores(dx),
        left,
        right,
        da,
        db,
        spaces={0: pltpu.SMEM},
    )
    back_send = back_send.reshape(CH, 2 * SUB, CH)
    back = exchange(back_send)
    coef, normed, zhat, partial, early = call(
        output_kernel,
        [struct((4 * CH, CELLS), BF16), narrow, narrow, wide, struct((3 * CH, CH), F32)],
        pair,
        grad_out,
        pair_mask,
        in_gain,
        in_bias,
        x_gain,
        x_bias,
        in_proj,
        w_gate,
        w_out,
        x_recv,
        back_send,
        scratch=[tiles],
        flops=500_000_000,
        fetched=range(10),
        hbm=(11,),
    )
    weights, d_normed = call(
        project_kernel,
        [one, wide],
        back,
        in_proj,
        coef,
        normed,
        zhat,
        partial,
        early,
        scratch=[
            pairs_of_tiles,
            tiles,
            pltpu.VMEM((CH, CELLS), F32),
            pltpu.SemaphoreType.DMA,
        ],
        hbm_outs=(1,),
    )
    weights = exchange(weights.reshape(PARTS, PART, CH), FLAT)
    (grad_pair,) = call(
        pair_kernel,
        [struct((T, T, CH), BF16)],
        d_normed,
        pair,
        in_gain,
        flops=500_000_000,
        fetched=range(3),
    )
    (totals,) = call(
        total_kernel, [struct((PEERS, PART, CH), BF16)], weights
    )
    totals = exchange(totals, UPRIGHT)
    (totals,) = call(
        total_kernel, [struct((PARTS, PART, CH), BF16)], totals, grad_pair, hbm=(1,)
    )
    totals = exchange(totals, FLAT).reshape(CH, SUB, CH)
    g_in, g_gate, g_out, ln_in, inner = call(
        unpack_kernel,
        [struct((CH, 4 * CH), F32), square, square, struct((2, CH), F32), struct((2, CH), F32)],
        totals,
        scratch=[tiles],
    )
    return grad_pair, g_in, g_gate, g_out, ln_in, inner


def solution(mesh):
    fine = Mesh(mesh.devices.reshape(SIZES), AXES)
    cells = P(ROW, COL + ("depth",), None)
    return jax.shard_map(
        per_device,
        mesh=fine,
        in_specs=(cells, cells, P(ROW, COL + ("depth",))) + (P(),) * 7,
        out_specs=(cells,) + (P(),) * 5,
        check_vma=False,
    )
```

```python
import itertools

import jax
import jax.numpy as jnp
from jax import lax
from jax.experimental import pallas as pl
from jax.experimental.pallas import tpu as pltpu
from jax.sharding import Mesh
from jax.sharding import PartitionSpec as P

F32 = jnp.float32
BF16 = jnp.bfloat16
T = 32
CH = 128
CELLS = T * T
SUB = 8
GROUPS = T // SUB
ROW = ("y", "z_lo")
COL = ("x", "z_hi")
SIZES = (4, 4, 4, 2, 2)
AXES = ROW + COL + ("depth",)
PLANE = ("z_lo", "y", "x", "z_hi")
FLAT = ("depth", "y", "x")
UPRIGHT = ("z_lo", "z_hi")
ORIGINS = {PLANE: (3, 2, 3, 1, 0), FLAT: (2, 0, 2, 0, 1), UPRIGHT: (0, 0, 0, 1, 0)}
PARTS = 32
PEERS = 8
PART = CELLS // PARTS


def groups(axes):
    sizes = dict(zip(AXES, SIZES))
    origin = dict(zip(AXES, ORIGINS[axes]))
    rest = [axis for axis in AXES if axis not in axes]
    listed = []
    for outer in itertools.product(*(range(sizes[axis]) for axis in rest)):
        members = []
        for inner in itertools.product(*(range(sizes[axis]) for axis in axes)):
            place = dict(zip(rest, outer))
            for axis, index in zip(axes, inner):
                place[axis] = (index + origin[axis]) % sizes[axis]
            member = 0
            for axis in AXES:
                member = member * sizes[axis] + place[axis]
            members.append(member)
        listed.append(members)
    return listed


def call(kernel, outs, *args, scratch=(), flops=2_000_000, spaces=None, fetched=(), hbm=(), hbm_outs=()):
    spaces = spaces or {}
    fetched = tuple(fetched)
    hbm = fetched + tuple(hbm)
    count = len(args)
    specs = [
        pl.BlockSpec(memory_space=pltpu.HBM if i in hbm else spaces.get(i, pltpu.VMEM))
        for i in range(count)
    ]
    moved = sum(a.size * a.dtype.itemsize for a in args)
    moved += sum(o.size * o.dtype.itemsize for o in outs)
    args = [
        pltpu.with_memory_space_constraint(a, pltpu.HBM) if i in hbm else a
        for i, a in enumerate(args)
    ]

    def body(*refs):
        if not fetched:
            return kernel(*refs)
        local = refs[len(refs) - 1 - len(fetched) : -1]
        refs, sems = refs[: len(refs) - 1 - len(fetched)], refs[-1]
        inputs = list(refs[:count])
        copies = [
            pltpu.make_async_copy(inputs[i], target, sems.at[place])
            for place, (i, target) in enumerate(zip(fetched, local))
        ]
        for copy in copies:
            copy.start()
        for copy in copies:
            copy.wait()
        for i, target in zip(fetched, local):
            inputs[i] = target
        return kernel(*inputs, *refs[count:])

    extra = [pltpu.VMEM(args[i].shape, args[i].dtype) for i in fetched]
    if fetched:
        extra.append(pltpu.SemaphoreType.DMA((len(fetched),)))
    return pl.pallas_call(
        body,
        out_shape=[pltpu.HBM(o.shape, o.dtype) if i in hbm_outs else o for i, o in enumerate(outs)],
        in_specs=specs,
        out_specs=[
            pl.BlockSpec(memory_space=pltpu.HBM if i in hbm_outs else pltpu.VMEM)
            for i in range(len(outs))
        ],
        scratch_shapes=list(scratch) + extra,
        compiler_params=pltpu.CompilerParams(vmem_limit_bytes=32 * 1024 * 1024),
        cost_estimate=pl.CostEstimate(flops=flops, bytes_accessed=moved, transcendentals=0),
    )(*args)


def struct(shape, dtype):
    return jax.ShapeDtypeStruct(shape, dtype)


def column(row):
    return jnp.transpose(jnp.broadcast_to(row, (CH, CH)))[:, :1]


def dot(a, b, ca, cb):
    return lax.dot_general(a, b, (((ca,), (cb,)), ((), ())), preferred_element_type=F32)


def channel_major(ref):
    chunks = []
    for s in range(SUB):
        block = jnp.concatenate([ref[SUB * g + s] for g in range(GROUPS)], axis=0)
        chunks.append(jnp.transpose(block.astype(F32)))
    return jnp.concatenate(chunks, axis=1)


def to_tiles(value, scratch, first, stride):
    for s in range(SUB):
        scratch[pl.ds(first + s, CH, stride=stride), :] = value[:, s * CH : (s + 1) * CH]


def from_tiles(scratch, first, stride):
    return jnp.concatenate(
        [scratch[pl.ds(first + s, CH, stride=stride), :] for s in range(SUB)], axis=1
    )


def norm(value):
    centre = value - jnp.mean(value, axis=0, keepdims=True)
    inverse = lax.rsqrt(jnp.mean(centre * centre, axis=0, keepdims=True) + 1e-05)
    return centre * inverse, inverse


def norm_back(tangent, scaled, inverse):
    first = jnp.mean(tangent, axis=0, keepdims=True)
    second = jnp.mean(tangent * scaled, axis=0, keepdims=True)
    return inverse * (tangent - first - scaled * second)


def swap_groups(parts):
    a, b, c, d = parts
    axis = a.ndim - 1
    lane = lax.broadcasted_iota(jnp.int32, a.shape, axis)
    low = lane < 64
    even = (lane & 32) == 0
    a, c = jnp.where(low, a, pltpu.roll(c, 64, axis)), jnp.where(low, pltpu.roll(a, 64, axis), c)
    b, d = jnp.where(low, b, pltpu.roll(d, 64, axis)), jnp.where(low, pltpu.roll(b, 64, axis), d)
    a, b = jnp.where(even, a, pltpu.roll(b, 32, axis)), jnp.where(even, pltpu.roll(a, 96, axis), b)
    c, d = jnp.where(even, c, pltpu.roll(d, 32, axis)), jnp.where(even, pltpu.roll(c, 96, axis), d)
    return a, b, c, d


def to_matrix(tiles):
    blocks = tiles.shape[0]
    halves = []
    for half in range(2):
        parts = [tiles[:, 2 * part + half].astype(F32) for part in range(4)]
        rows = jnp.stack(swap_groups(parts), axis=1)
        halves.append(rows.reshape(blocks * T, CH))
    return jnp.concatenate(halves, axis=1)


def from_matrix(matrix):
    blocks = matrix.shape[0] // T
    halves = []
    for half in range(2):
        rows = matrix[:, half * CH : (half + 1) * CH].reshape(blocks, GROUPS, SUB, CH)
        halves.append(swap_groups([rows[:, g] for g in range(GROUPS)]))
    return jnp.stack([halves[half][part] for part in range(4) for half in range(2)], axis=1)


def normalise(pair, gain, bias):
    scaled, inverse = norm(channel_major(pair))
    return scaled, inverse, (scaled * column(gain[...]) + column(bias[...])).astype(BF16)


def factors_of(normed, mask, in_proj):
    proj = dot(in_proj[...], normed, 0, 0)
    flags = mask[...].astype(F32)
    tile = jnp.concatenate([flags[SUB * g : SUB * (g + 1)] for g in range(GROUPS)], axis=1)
    m = jnp.concatenate([tile[s : s + 1] for s in range(SUB)], axis=1)
    sides = []
    for side in range(2):
        val = proj[2 * side * CH : (2 * side + 1) * CH]
        sig = jax.nn.sigmoid(proj[(2 * side + 1) * CH : (2 * side + 2) * CH])
        gated = sig * m
        sides.append((gated, gated * val, 1.0 - sig))
    return sides


def factors_kernel(
    pair, grad_out, mask, gain, bias, x_gain, in_proj, w_gate, w_out, send, tangent, scratch
):
    normed = normalise(pair, gain, bias)[2]
    for side, (_, factor, _) in enumerate(factors_of(normed, mask, in_proj)):
        to_tiles(factor, scratch, side * SUB, 2 * SUB)
    send[...] = scratch[...].reshape(CH, 2 * SUB, CH).astype(BF16)
    d_out_proj, _ = gated_grad(grad_out, normed, w_gate)
    tangent[...] = dot(w_out[...], d_out_proj, 1, 0) * column(x_gain[...])


def gated_grad(grad_out, normed, w_gate):
    gate = jax.nn.sigmoid(dot(w_gate[...], normed, 0, 0))
    moved = channel_major(grad_out) * gate
    return moved.astype(BF16), moved * (1.0 - gate)


def product_theirs_kernel(parity, own, left_out, theirs):
    other = 1 - lax.bitwise_and(parity[0], 1)
    left = to_matrix(own[:, :, :, :, :SUB].reshape(16, 8, SUB, CH)).astype(BF16)
    left_out[...] = left
    right = to_matrix(own[:, pl.ds(other, 1), :, :, SUB:].reshape(8, 8, SUB, CH)).astype(BF16)
    theirs[...] = from_matrix(dot(left, right, 1, 1)).reshape(CH, SUB, CH).astype(BF16)


def product_mine_kernel(parity, own, left, right_out, mine):
    place = lax.bitwise_and(parity[0], 1)
    right_out[...] = to_matrix(own[:, :, :, :, SUB:].reshape(16, 8, SUB, CH)).astype(BF16)
    right = to_matrix(own[:, pl.ds(place, 1), :, :, SUB:].reshape(8, 8, SUB, CH)).astype(BF16)
    mine[...] = from_matrix(dot(left[...], right, 1, 1)).reshape(CH, SUB, CH)


def product_kernel(mine, got, send):
    send[...] = (mine[...] + got[...].astype(F32)).astype(BF16)


def inner_kernel(recv, tangent, send, scratch):
    scratch[...] = recv[...].astype(F32).reshape(CELLS, CH)
    scaled, inverse = norm(from_tiles(scratch, 0, SUB))
    to_tiles(norm_back(tangent[...], scaled, inverse), scratch, 0, SUB)
    send[...] = scratch[...].reshape(CH, SUB, CH).astype(BF16)


def sums(first, second, place):
    lane = lax.broadcasted_iota(jnp.int32, (CH, CH), 1)
    a = jnp.sum(first, axis=1, keepdims=True)
    b = jnp.sum(second, axis=1, keepdims=True)
    return jnp.where(lane == place, a, jnp.where(lane == place + 1, b, 0.0))


def output_kernel(
    pair,
    grad_out,
    mask,
    gain,
    bias,
    x_gain,
    x_bias,
    in_proj,
    w_gate,
    w_out,
    x_recv,
    after,
    coef,
    normed_out,
    zhat,
    partial,
    early,
    scratch,
):
    scaled, _, normed = normalise(pair, gain, bias)
    zhat[...] = scaled.astype(BF16)
    normed_out[...] = normed
    for side, (gated, factor, rest) in enumerate(factors_of(normed, mask, in_proj)):
        coef[2 * side * CH : (2 * side + 1) * CH] = gated.astype(BF16)
        coef[(2 * side + 1) * CH : (2 * side + 2) * CH] = (factor * rest).astype(BF16)
    d_out_proj, slope = gated_grad(grad_out, normed, w_gate)
    d_xnorm = dot(w_out[...], d_out_proj, 1, 0)
    scratch[...] = x_recv[...].astype(F32).reshape(CELLS, CH)
    xhat, _ = norm(from_tiles(scratch, 0, SUB))
    xnorm = (xhat * column(x_gain[...]) + column(x_bias[...])).astype(BF16)
    d_gate_pre = (slope * dot(w_out[...], xnorm, 0, 0)).astype(BF16)
    early[0:CH] = dot(normed, d_gate_pre, 1, 1)
    early[CH : 2 * CH] = dot(xnorm, d_out_proj, 1, 1)
    early[2 * CH :] = sums(d_xnorm * xhat, d_xnorm, 2)
    partial[...] = dot(w_gate[...], d_gate_pre, 1, 0)


def back_mine_kernel(parity, own, left, right, da, db):
    place = lax.bitwise_and(parity[0], 1)
    grad = to_matrix(own[...].reshape(16, 8, SUB, CH)).astype(BF16)
    da[...] = dot(grad, right[:, pl.ds(place, 1)].reshape(8 * T, 2 * CH), 1, 0)
    db[...] = from_matrix(dot(grad, left[...], 0, 0)).astype(BF16)


def back_kernel(parity, other, left, right, da_mine, db_mine, send):
    place = lax.bitwise_and(parity[0], 1)
    grad = to_matrix(other[...].reshape(16, 8, SUB, CH)).astype(BF16)
    da = da_mine[...] + dot(grad, right[:, pl.ds(1 - place, 1)].reshape(8 * T, 2 * CH), 1, 0)
    db = from_matrix(dot(grad, left[...], 0, 0)).astype(BF16)
    send[:, :, :, :, :SUB] = from_matrix(da).reshape(2, 2, 4, 8, SUB, CH).astype(BF16)
    send[:, pl.ds(place, 1), :, :, SUB:] = db_mine[...].reshape(2, 1, 4, 8, SUB, CH)
    send[:, pl.ds(1 - place, 1), :, :, SUB:] = db.reshape(2, 1, 4, 8, SUB, CH)


def project_kernel(
    recv, in_proj, coef, normed, zhat, partial, early, send, d_normed, scratch, packed
):
    scratch[...] = recv[...].astype(F32).reshape(2 * CELLS, CH)
    da = from_tiles(scratch, 0, 2 * SUB)
    db = from_tiles(scratch, SUB, 2 * SUB)
    d_proj = jnp.concatenate(
        [
            (grad * coef[part * CH : (part + 1) * CH].astype(F32)).astype(BF16)
            for part, grad in enumerate((da, da, db, db))
        ],
        axis=0,
    )
    g_in = dot(normed[...], d_proj, 1, 1)
    grad = dot(in_proj[...], d_proj, 1, 0) + partial[...]
    d_normed[...] = grad
    for part in range(4):
        packed[pl.ds(part, CH, stride=SUB), :] = g_in[:, part * CH : (part + 1) * CH]
    packed[pl.ds(4, CH, stride=SUB), :] = early[0:CH]
    packed[pl.ds(5, CH, stride=SUB), :] = early[CH : 2 * CH]
    packed[pl.ds(6, CH, stride=SUB), :] = early[2 * CH :] + sums(
        grad * zhat[...].astype(F32), grad, 0
    )
    packed[pl.ds(7, CH, stride=SUB), :] = jnp.zeros((CH, CH), F32)
    send[...] = packed[...].reshape(CH, SUB, CH).astype(BF16)


def pair_kernel(d_normed, pair, gain, out):
    scaled, inverse = norm(channel_major(pair))
    grad = norm_back(d_normed[...] * column(gain[...]), scaled, inverse)
    for s in range(SUB):
        block = jnp.transpose(grad[:, s * CH : (s + 1) * CH]).astype(BF16)
        for g in range(GROUPS):
            out[SUB * g + s] = block[g * T : (g + 1) * T]


def total_kernel(recv, *refs):
    send = refs[-1]
    total = jnp.sum(recv[...].astype(F32), axis=0, keepdims=True)
    send[...] = jnp.broadcast_to(total, send.shape).astype(BF16)


def unpack_kernel(totals, g_in, g_gate, g_out, ln_in, inner, scratch):
    scratch[...] = totals[...].astype(F32).reshape(CELLS, CH)
    for part in range(4):
        g_in[:, part * CH : (part + 1) * CH] = scratch[pl.ds(part, CH, stride=SUB), :]
    g_gate[...] = scratch[pl.ds(4, CH, stride=SUB), :]
    g_out[...] = scratch[pl.ds(5, CH, stride=SUB), :]
    norms = jnp.transpose(scratch[pl.ds(6, CH, stride=SUB), :])
    ln_in[...] = norms[0:2]
    inner[...] = norms[2:4]


def swap_cores(value):
    return lax.ppermute(value, "depth", [(0, 1), (1, 0)])


def exchange(value, axes=PLANE):
    return lax.all_to_all(value, AXES, 0, 0, tiled=True, axis_index_groups=groups(axes))


def per_device(
    pair,
    grad_out,
    pair_mask,
    ln_in_gain,
    ln_in_bias,
    in_proj,
    w_gate,
    inner_norm_gain,
    inner_norm_bias,
    w_out,
):
    parity = lax.axis_index("depth").astype(jnp.int32).reshape(1)
    in_gain = ln_in_gain.reshape(1, CH)
    in_bias = ln_in_bias.reshape(1, CH)
    x_gain = inner_norm_gain.reshape(1, CH)
    x_bias = inner_norm_bias.reshape(1, CH)
    one = struct((CH, SUB, CH), BF16)
    two = struct((CH, 2 * SUB, CH), BF16)
    square = struct((CH, CH), F32)
    matrix = struct((16 * T, 2 * CH), BF16)
    wide = struct((CH, CELLS), F32)
    narrow = struct((CH, CELLS), BF16)
    tiles = pltpu.VMEM((CELLS, CH), F32)
    pairs_of_tiles = pltpu.VMEM((2 * CELLS, CH), F32)

    factors, tangent = call(
        factors_kernel,
        [two, wide],
        pair,
        grad_out,
        pair_mask,
        in_gain,
        in_bias,
        x_gain,
        in_proj,
        w_gate,
        w_out,
        scratch=[pairs_of_tiles],
        fetched=range(9),
    )
    factors, parity = lax.optimization_barrier((factors, parity))
    factors = exchange(factors).reshape(2, 2, 4, 8, 2 * SUB, CH)
    left, x_theirs = call(
        product_theirs_kernel, [matrix, one], parity, factors, spaces={0: pltpu.SMEM}
    )
    x_got = swap_cores(x_theirs)
    right, x_mine = call(
        product_mine_kernel,
        [matrix, struct((CH, SUB, CH), F32)],
        parity,
        factors,
        left,
        spaces={0: pltpu.SMEM},
    )
    right = right.reshape(2, 2, 4 * T, 2 * CH)
    (x_send,) = call(product_kernel, [one], x_mine, x_got)
    x_recv = exchange(x_send)
    (dx_send,) = call(inner_kernel, [one], x_recv, tangent, scratch=[tiles])
    dx = exchange(dx_send)
    da, db = call(
        back_mine_kernel,
        [struct((16 * T, 2 * CH), F32), struct((8, 8, SUB, CH), BF16)],
        parity,
        dx,
        left,
        right,
        spaces={0: pltpu.SMEM},
    )
    (back_send,) = call(
        back_kernel,
        [struct((2, 2, 4, 8, 2 * SUB, CH), BF16)],
        parity,
        swap_cores(dx),
        left,
        right,
        da,
        db,
        spaces={0: pltpu.SMEM},
    )
    back_send = back_send.reshape(CH, 2 * SUB, CH)
    back = exchange(back_send)
    coef, normed, zhat, partial, early = call(
        output_kernel,
        [struct((4 * CH, CELLS), BF16), narrow, narrow, wide, struct((3 * CH, CH), F32)],
        pair,
        grad_out,
        pair_mask,
        in_gain,
        in_bias,
        x_gain,
        x_bias,
        in_proj,
        w_gate,
        w_out,
        x_recv,
        back_send,
        scratch=[tiles],
        flops=500_000_000,
        fetched=range(10),
        hbm=(11,),
    )
    weights, d_normed = call(
        project_kernel,
        [one, wide],
        back,
        in_proj,
        coef,
        normed,
        zhat,
        partial,
        early,
        scratch=[
            pairs_of_tiles,
            tiles,
        ],
    )
    weights = exchange(weights.reshape(PARTS, PART, CH), FLAT)
    (grad_pair,) = call(
        pair_kernel,
        [struct((T, T, CH), BF16)],
        d_normed,
        pair,
        in_gain,
        flops=500_000_000,
        fetched=(1, 2),
    )
    (totals,) = call(
        total_kernel, [struct((PEERS, PART, CH), BF16)], weights
    )
    totals = exchange(totals, UPRIGHT)
    (totals,) = call(
        total_kernel, [struct((PARTS, PART, CH), BF16)], totals, grad_pair, hbm=(1,)
    )
    totals = exchange(totals, FLAT).reshape(CH, SUB, CH)
    g_in, g_gate, g_out, ln_in, inner = call(
        unpack_kernel,
        [struct((CH, 4 * CH), F32), square, square, struct((2, CH), F32), struct((2, CH), F32)],
        totals,
        scratch=[tiles],
    )
    return grad_pair, g_in, g_gate, g_out, ln_in, inner


def solution(mesh):
    fine = Mesh(mesh.devices.reshape(SIZES), AXES)
    cells = P(ROW, COL + ("depth",), None)
    return jax.shard_map(
        per_device,
        mesh=fine,
        in_specs=(cells, cells, P(ROW, COL + ("depth",))) + (P(),) * 7,
        out_specs=(cells,) + (P(),) * 5,
        check_vma=False,
    )
```

```python
import itertools

import jax
import jax.numpy as jnp
from jax import lax
from jax.experimental import pallas as pl
from jax.experimental.pallas import tpu as pltpu
from jax.sharding import Mesh
from jax.sharding import PartitionSpec as P

F32 = jnp.float32
BF16 = jnp.bfloat16
T = 32
CH = 128
CELLS = T * T
SUB = 8
GROUPS = T // SUB
ROW = ("y", "z_lo")
COL = ("x", "z_hi")
SIZES = (4, 4, 4, 2, 2)
AXES = ROW + COL + ("depth",)
PLANE = ("z_lo", "y", "x", "z_hi")
FLAT = ("depth", "y", "x")
UPRIGHT = ("z_lo", "z_hi")
ORIGINS = {PLANE: (3, 2, 3, 1, 0), FLAT: (2, 0, 2, 0, 1), UPRIGHT: (0, 0, 0, 1, 0)}
PARTS = 32
PEERS = 8
PART = CELLS // PARTS


def groups(axes):
    sizes = dict(zip(AXES, SIZES))
    origin = dict(zip(AXES, ORIGINS[axes]))
    rest = [axis for axis in AXES if axis not in axes]
    listed = []
    for outer in itertools.product(*(range(sizes[axis]) for axis in rest)):
        members = []
        for inner in itertools.product(*(range(sizes[axis]) for axis in axes)):
            place = dict(zip(rest, outer))
            for axis, index in zip(axes, inner):
                place[axis] = (index + origin[axis]) % sizes[axis]
            member = 0
            for axis in AXES:
                member = member * sizes[axis] + place[axis]
            members.append(member)
        listed.append(members)
    return listed


def call(kernel, outs, *args, scratch=(), flops=2_000_000, spaces=None, fetched=(), hbm=(), hbm_outs=()):
    spaces = spaces or {}
    fetched = tuple(fetched)
    hbm = fetched + tuple(hbm)
    count = len(args)
    specs = [
        pl.BlockSpec(memory_space=pltpu.HBM if i in hbm else spaces.get(i, pltpu.VMEM))
        for i in range(count)
    ]
    moved = sum(a.size * a.dtype.itemsize for a in args)
    moved += sum(o.size * o.dtype.itemsize for o in outs)
    args = [
        pltpu.with_memory_space_constraint(a, pltpu.HBM) if i in hbm else a
        for i, a in enumerate(args)
    ]

    def body(*refs):
        if not fetched:
            return kernel(*refs)
        local = refs[len(refs) - 1 - len(fetched) : -1]
        refs, sems = refs[: len(refs) - 1 - len(fetched)], refs[-1]
        inputs = list(refs[:count])
        copies = [
            pltpu.make_async_copy(inputs[i], target, sems.at[place])
            for place, (i, target) in enumerate(zip(fetched, local))
        ]
        for copy in copies:
            copy.start()
        for copy in copies:
            copy.wait()
        for i, target in zip(fetched, local):
            inputs[i] = target
        return kernel(*inputs, *refs[count:])

    extra = [pltpu.VMEM(args[i].shape, args[i].dtype) for i in fetched]
    if fetched:
        extra.append(pltpu.SemaphoreType.DMA((len(fetched),)))
    return pl.pallas_call(
        body,
        out_shape=[pltpu.HBM(o.shape, o.dtype) if i in hbm_outs else o for i, o in enumerate(outs)],
        in_specs=specs,
        out_specs=[
            pl.BlockSpec(memory_space=pltpu.HBM if i in hbm_outs else pltpu.VMEM)
            for i in range(len(outs))
        ],
        scratch_shapes=list(scratch) + extra,
        compiler_params=pltpu.CompilerParams(vmem_limit_bytes=32 * 1024 * 1024),
        cost_estimate=pl.CostEstimate(flops=flops, bytes_accessed=moved, transcendentals=0),
    )(*args)


def struct(shape, dtype):
    return jax.ShapeDtypeStruct(shape, dtype)


def column(row):
    return jnp.transpose(jnp.broadcast_to(row, (CH, CH)))[:, :1]


def dot(a, b, ca, cb):
    return lax.dot_general(a, b, (((ca,), (cb,)), ((), ())), preferred_element_type=F32)


def channel_major(ref):
    chunks = []
    for s in range(SUB):
        block = jnp.concatenate([ref[SUB * g + s] for g in range(GROUPS)], axis=0)
        chunks.append(jnp.transpose(block.astype(F32)))
    return jnp.concatenate(chunks, axis=1)


def to_tiles(value, scratch, first, stride):
    for s in range(SUB):
        scratch[pl.ds(first + s, CH, stride=stride), :] = value[:, s * CH : (s + 1) * CH]


def from_tiles(scratch, first, stride):
    return jnp.concatenate(
        [scratch[pl.ds(first + s, CH, stride=stride), :] for s in range(SUB)], axis=1
    )


def norm(value):
    centre = value - jnp.mean(value, axis=0, keepdims=True)
    inverse = lax.rsqrt(jnp.mean(centre * centre, axis=0, keepdims=True) + 1e-05)
    return centre * inverse, inverse


def norm_back(tangent, scaled, inverse):
    first = jnp.mean(tangent, axis=0, keepdims=True)
    second = jnp.mean(tangent * scaled, axis=0, keepdims=True)
    return inverse * (tangent - first - scaled * second)


def swap_groups(parts):
    a, b, c, d = parts
    axis = a.ndim - 1
    lane = lax.broadcasted_iota(jnp.int32, a.shape, axis)
    low = lane < 64
    even = (lane & 32) == 0
    a, c = jnp.where(low, a, pltpu.roll(c, 64, axis)), jnp.where(low, pltpu.roll(a, 64, axis), c)
    b, d = jnp.where(low, b, pltpu.roll(d, 64, axis)), jnp.where(low, pltpu.roll(b, 64, axis), d)
    a, b = jnp.where(even, a, pltpu.roll(b, 32, axis)), jnp.where(even, pltpu.roll(a, 96, axis), b)
    c, d = jnp.where(even, c, pltpu.roll(d, 32, axis)), jnp.where(even, pltpu.roll(c, 96, axis), d)
    return a, b, c, d


def to_matrix(tiles):
    blocks = tiles.shape[0]
    halves = []
    for half in range(2):
        parts = [tiles[:, 2 * part + half].astype(F32) for part in range(4)]
        rows = jnp.stack(swap_groups(parts), axis=1)
        halves.append(rows.reshape(blocks * T, CH))
    return jnp.concatenate(halves, axis=1)


def from_matrix(matrix):
    blocks = matrix.shape[0] // T
    halves = []
    for half in range(2):
        rows = matrix[:, half * CH : (half + 1) * CH].reshape(blocks, GROUPS, SUB, CH)
        halves.append(swap_groups([rows[:, g] for g in range(GROUPS)]))
    return jnp.stack([halves[half][part] for part in range(4) for half in range(2)], axis=1)


def normalise(pair, gain, bias):
    scaled, inverse = norm(channel_major(pair))
    return scaled, inverse, (scaled * column(gain[...]) + column(bias[...])).astype(BF16)


def factors_of(normed, mask, in_proj):
    proj = dot(in_proj[...], normed, 0, 0)
    flags = mask[...].astype(F32)
    tile = jnp.concatenate([flags[SUB * g : SUB * (g + 1)] for g in range(GROUPS)], axis=1)
    m = jnp.concatenate([tile[s : s + 1] for s in range(SUB)], axis=1)
    sides = []
    for side in range(2):
        val = proj[2 * side * CH : (2 * side + 1) * CH]
        sig = jax.nn.sigmoid(proj[(2 * side + 1) * CH : (2 * side + 2) * CH])
        gated = sig * m
        sides.append((gated, gated * val, 1.0 - sig))
    return sides


def factors_kernel(
    pair, grad_out, mask, gain, bias, x_gain, in_proj, w_gate, w_out, send, tangent, scratch
):
    normed = normalise(pair, gain, bias)[2]
    for side, (_, factor, _) in enumerate(factors_of(normed, mask, in_proj)):
        to_tiles(factor, scratch, side * SUB, 2 * SUB)
    send[...] = scratch[...].reshape(CH, 2 * SUB, CH).astype(BF16)
    d_out_proj, _ = gated_grad(grad_out, normed, w_gate)
    tangent[...] = dot(w_out[...], d_out_proj, 1, 0) * column(x_gain[...])


def gated_grad(grad_out, normed, w_gate):
    gate = jax.nn.sigmoid(dot(w_gate[...], normed, 0, 0))
    moved = channel_major(grad_out) * gate
    return moved.astype(BF16), moved * (1.0 - gate)


def product_theirs_kernel(parity, own, left_out, theirs):
    other = 1 - lax.bitwise_and(parity[0], 1)
    left = to_matrix(own[:, :, :, :, :SUB].reshape(16, 8, SUB, CH)).astype(BF16)
    left_out[...] = left
    right = to_matrix(own[:, pl.ds(other, 1), :, :, SUB:].reshape(8, 8, SUB, CH)).astype(BF16)
    theirs[...] = from_matrix(dot(left, right, 1, 1)).reshape(CH, SUB, CH).astype(BF16)


def product_mine_kernel(parity, own, left, right_out, mine):
    place = lax.bitwise_and(parity[0], 1)
    right_out[...] = to_matrix(own[:, :, :, :, SUB:].reshape(16, 8, SUB, CH)).astype(BF16)
    right = to_matrix(own[:, pl.ds(place, 1), :, :, SUB:].reshape(8, 8, SUB, CH)).astype(BF16)
    mine[...] = from_matrix(dot(left[...], right, 1, 1)).reshape(CH, SUB, CH)


def product_kernel(mine, got, send):
    send[...] = (mine[...] + got[...].astype(F32)).astype(BF16)


def inner_kernel(recv, tangent, send, scratch):
    scratch[...] = recv[...].astype(F32).reshape(CELLS, CH)
    scaled, inverse = norm(from_tiles(scratch, 0, SUB))
    to_tiles(norm_back(tangent[...], scaled, inverse), scratch, 0, SUB)
    send[...] = scratch[...].reshape(CH, SUB, CH).astype(BF16)


def sums(first, second, place):
    lane = lax.broadcasted_iota(jnp.int32, (CH, CH), 1)
    a = jnp.sum(first, axis=1, keepdims=True)
    b = jnp.sum(second, axis=1, keepdims=True)
    return jnp.where(lane == place, a, jnp.where(lane == place + 1, b, 0.0))


def output_kernel(
    pair,
    grad_out,
    mask,
    gain,
    bias,
    x_gain,
    x_bias,
    in_proj,
    w_gate,
    w_out,
    x_recv,
    after,
    coef,
    normed_out,
    zhat,
    partial,
    early,
    scratch,
):
    scaled, _, normed = normalise(pair, gain, bias)
    zhat[...] = scaled.astype(BF16)
    normed_out[...] = normed
    for side, (gated, factor, rest) in enumerate(factors_of(normed, mask, in_proj)):
        coef[2 * side * CH : (2 * side + 1) * CH] = gated.astype(BF16)
        coef[(2 * side + 1) * CH : (2 * side + 2) * CH] = (factor * rest).astype(BF16)
    d_out_proj, slope = gated_grad(grad_out, normed, w_gate)
    d_xnorm = dot(w_out[...], d_out_proj, 1, 0)
    scratch[...] = x_recv[...].astype(F32).reshape(CELLS, CH)
    xhat, _ = norm(from_tiles(scratch, 0, SUB))
    xnorm = (xhat * column(x_gain[...]) + column(x_bias[...])).astype(BF16)
    d_gate_pre = (slope * dot(w_out[...], xnorm, 0, 0)).astype(BF16)
    early[0:CH] = dot(normed, d_gate_pre, 1, 1)
    early[CH : 2 * CH] = dot(xnorm, d_out_proj, 1, 1)
    early[2 * CH :] = sums(d_xnorm * xhat, d_xnorm, 2)
    partial[...] = dot(w_gate[...], d_gate_pre, 1, 0)


def back_mine_kernel(parity, own, left, right, da, db):
    place = lax.bitwise_and(parity[0], 1)
    grad = to_matrix(own[...].reshape(16, 8, SUB, CH)).astype(BF16)
    da[...] = dot(grad, right[:, pl.ds(place, 1)].reshape(8 * T, 2 * CH), 1, 0)
    db[...] = from_matrix(dot(grad, left[...], 0, 0)).astype(BF16)


def back_kernel(parity, other, left, right, da_mine, db_mine, send):
    place = lax.bitwise_and(parity[0], 1)
    grad = to_matrix(other[...].reshape(16, 8, SUB, CH)).astype(BF16)
    da = da_mine[...] + dot(grad, right[:, pl.ds(1 - place, 1)].reshape(8 * T, 2 * CH), 1, 0)
    db = from_matrix(dot(grad, left[...], 0, 0)).astype(BF16)
    send[:, :, :, :, :SUB] = from_matrix(da).reshape(2, 2, 4, 8, SUB, CH).astype(BF16)
    send[:, pl.ds(place, 1), :, :, SUB:] = db_mine[...].reshape(2, 1, 4, 8, SUB, CH)
    send[:, pl.ds(1 - place, 1), :, :, SUB:] = db.reshape(2, 1, 4, 8, SUB, CH)


def project_kernel(
    recv, in_proj, coef, normed, zhat, partial, early, send, d_normed, scratch, packed, kept, sem
):
    scratch[...] = recv[...].astype(F32).reshape(2 * CELLS, CH)
    da = from_tiles(scratch, 0, 2 * SUB)
    db = from_tiles(scratch, SUB, 2 * SUB)
    d_proj = jnp.concatenate(
        [
            (grad * coef[part * CH : (part + 1) * CH].astype(F32)).astype(BF16)
            for part, grad in enumerate((da, da, db, db))
        ],
        axis=0,
    )
    g_in = dot(normed[...], d_proj, 1, 1)
    grad = dot(in_proj[...], d_proj, 1, 0) + partial[...]
    kept[...] = grad
    copy = pltpu.make_async_copy(kept, d_normed, sem)
    copy.start()
    for part in range(4):
        packed[pl.ds(part, CH, stride=SUB), :] = g_in[:, part * CH : (part + 1) * CH]
    packed[pl.ds(4, CH, stride=SUB), :] = early[0:CH]
    packed[pl.ds(5, CH, stride=SUB), :] = early[CH : 2 * CH]
    packed[pl.ds(6, CH, stride=SUB), :] = early[2 * CH :] + sums(
        grad * zhat[...].astype(F32), grad, 0
    )
    packed[pl.ds(7, CH, stride=SUB), :] = jnp.zeros((CH, CH), F32)
    send[...] = packed[...].reshape(CH, SUB, CH).astype(BF16)
    copy.wait()


def pair_kernel(d_normed, pair, gain, out):
    scaled, inverse = norm(channel_major(pair))
    grad = norm_back(d_normed[...] * column(gain[...]), scaled, inverse)
    for s in range(SUB):
        block = jnp.transpose(grad[:, s * CH : (s + 1) * CH]).astype(BF16)
        for g in range(GROUPS):
            out[SUB * g + s] = block[g * T : (g + 1) * T]


def total_kernel(recv, *refs):
    send = refs[-1]
    total = jnp.sum(recv[...].astype(F32), axis=0, keepdims=True)
    send[...] = jnp.broadcast_to(total, send.shape).astype(BF16)


def unpack_kernel(totals, g_in, g_gate, g_out, ln_in, inner, scratch):
    scratch[...] = totals[...].astype(F32).reshape(CELLS, CH)
    for part in range(4):
        g_in[:, part * CH : (part + 1) * CH] = scratch[pl.ds(part, CH, stride=SUB), :]
    g_gate[...] = scratch[pl.ds(4, CH, stride=SUB), :]
    g_out[...] = scratch[pl.ds(5, CH, stride=SUB), :]
    norms = jnp.transpose(scratch[pl.ds(6, CH, stride=SUB), :])
    ln_in[...] = norms[0:2]
    inner[...] = norms[2:4]


def swap_cores(value):
    return lax.ppermute(value, "depth", [(0, 1), (1, 0)])


def exchange(value, axes=PLANE):
    return lax.all_to_all(value, AXES, 0, 0, tiled=True, axis_index_groups=groups(axes))


def per_device(
    pair,
    grad_out,
    pair_mask,
    ln_in_gain,
    ln_in_bias,
    in_proj,
    w_gate,
    inner_norm_gain,
    inner_norm_bias,
    w_out,
):
    parity = lax.axis_index("depth").astype(jnp.int32).reshape(1)
    in_gain = ln_in_gain.reshape(1, CH)
    in_bias = ln_in_bias.reshape(1, CH)
    x_gain = inner_norm_gain.reshape(1, CH)
    x_bias = inner_norm_bias.reshape(1, CH)
    one = struct((CH, SUB, CH), BF16)
    two = struct((CH, 2 * SUB, CH), BF16)
    square = struct((CH, CH), F32)
    matrix = struct((16 * T, 2 * CH), BF16)
    wide = struct((CH, CELLS), F32)
    narrow = struct((CH, CELLS), BF16)
    tiles = pltpu.VMEM((CELLS, CH), F32)
    pairs_of_tiles = pltpu.VMEM((2 * CELLS, CH), F32)

    factors, tangent = call(
        factors_kernel,
        [two, wide],
        pair,
        grad_out,
        pair_mask,
        in_gain,
        in_bias,
        x_gain,
        in_proj,
        w_gate,
        w_out,
        scratch=[pairs_of_tiles],
        fetched=range(9),
    )
    factors, parity = lax.optimization_barrier((factors, parity))
    factors = exchange(factors).reshape(2, 2, 4, 8, 2 * SUB, CH)
    left, x_theirs = call(
        product_theirs_kernel, [matrix, one], parity, factors, spaces={0: pltpu.SMEM}
    )
    x_got = swap_cores(x_theirs)
    right, x_mine = call(
        product_mine_kernel,
        [matrix, struct((CH, SUB, CH), F32)],
        parity,
        factors,
        left,
        spaces={0: pltpu.SMEM},
    )
    right = right.reshape(2, 2, 4 * T, 2 * CH)
    (x_send,) = call(product_kernel, [one], x_mine, x_got)
    x_recv = exchange(x_send)
    (dx_send,) = call(inner_kernel, [one], x_recv, tangent, scratch=[tiles])
    dx = exchange(dx_send)
    da, db = call(
        back_mine_kernel,
        [struct((16 * T, 2 * CH), F32), struct((8, 8, SUB, CH), BF16)],
        parity,
        dx,
        left,
        right,
        spaces={0: pltpu.SMEM},
    )
    (back_send,) = call(
        back_kernel,
        [struct((2, 2, 4, 8, 2 * SUB, CH), BF16)],
        parity,
        swap_cores(dx),
        left,
        right,
        da,
        db,
        spaces={0: pltpu.SMEM},
    )
    back_send = back_send.reshape(CH, 2 * SUB, CH)
    back = exchange(back_send)
    coef, normed, zhat, partial, early = call(
        output_kernel,
        [struct((4 * CH, CELLS), BF16), narrow, narrow, wide, struct((3 * CH, CH), F32)],
        pair,
        grad_out,
        pair_mask,
        in_gain,
        in_bias,
        x_gain,
        x_bias,
        in_proj,
        w_gate,
        w_out,
        x_recv,
        back_send,
        scratch=[tiles],
        flops=500_000_000,
        fetched=range(10),
        hbm=(11,),
    )
    weights, d_normed = call(
        project_kernel,
        [one, wide],
        back,
        in_proj,
        coef,
        normed,
        zhat,
        partial,
        early,
        scratch=[
            pairs_of_tiles,
            tiles,
            pltpu.VMEM((CH, CELLS), F32),
            pltpu.SemaphoreType.DMA,
        ],
        hbm_outs=(1,),
    )
    weights = exchange(weights.reshape(PARTS, PART, CH), FLAT)
    (grad_pair,) = call(
        pair_kernel,
        [struct((T, T, CH), BF16)],
        d_normed,
        pair,
        in_gain,
        flops=500_000_000,
        fetched=range(3),
    )
    (totals,) = call(
        total_kernel, [struct((PEERS, PART, CH), BF16)], weights
    )
    totals = exchange(totals, UPRIGHT)
    (totals,) = call(
        total_kernel, [struct((PARTS, PART, CH), BF16)], totals, grad_pair, hbm=(1,)
    )
    totals = exchange(totals, FLAT).reshape(CH, SUB, CH)
    g_in, g_gate, g_out, ln_in, inner = call(
        unpack_kernel,
        [struct((CH, 4 * CH), F32), square, square, struct((2, CH), F32), struct((2, CH), F32)],
        totals,
        scratch=[tiles],
    )
    return grad_pair, g_in, g_gate, g_out, ln_in, inner


def solution(mesh):
    fine = Mesh(mesh.devices.reshape(SIZES), AXES)
    cells = P(ROW, COL + ("depth",), None)
    return jax.shard_map(
        per_device,
        mesh=fine,
        in_specs=(cells, cells, P(ROW, COL + ("depth",))) + (P(),) * 7,
        out_specs=(cells,) + (P(),) * 5,
        check_vma=False,
    )
```
